128 devices in a mesh: fsdp: 8 (over x, core), blk: 16 (over z, y).
Axes of the slice: x: 4, y: 4, z: 4, core: 2. Of those that a mesh axis runs over, the one named last changes fastest.
Arguments:
- grad: bfloat16 [48, 512, 8192], P('blk', 'fsdp'), may hold values from -6 to 6
- first_moment: bfloat16 [48, 8192, 512], P('fsdp', 'blk'), may hold values from -4 to 4
- second_moment: bfloat16 [48, 8192, 512], P('fsdp', 'blk'), may hold values from 0.049804688 to 2
- left_basis: bfloat16 [48, 8192, 512], P('fsdp', 'blk'), may hold values from -0.25 to 0.25
- right_basis: bfloat16 [48, 8192, 512], P('fsdp', 'blk'), may hold values from -0.25 to 0.25
- block_owner: int32 [48, 16], replicated, may hold values from 0 to 15, as said below
Outputs:
- update: bfloat16 [48, 512, 8192], P('blk', 'fsdp')
- new_first: bfloat16 [48, 8192, 512], P('fsdp', 'blk')
- new_second: bfloat16 [48, 8192, 512], P('fsdp', 'blk')
- owner_load: float32 [8, 16], P('fsdp', 'blk')
The draws below stay inside these ranges and needn't reach their ends.
Inputs may be any that keep to these rules, and one draw needn't show every extreme that they name: `block_owner`: within each column group, each owner is named by exactly 6 blocks, and the blocks of that group in the 3 bands of one blk index name each owner either 0 or 1 times.
All inputs are finite; a program needn't handle non-finite values.
Results may differ from the reference program's by a relative error of at most 0.0059.
Values may be sent and summed in bfloat16 or wider, within the bound.
A program may use at most 128 MiB of HBM per device.

```python
import math
import jax
import jax.numpy as jnp
from jax import lax

D = 8192
BS = 512
NB_DEV = 3
CB_DEV = 2
BLOCKS_DEV = 6
PER_PEER = 1
TARGETS = 6
BANDS = 48
N_FSDP = 8
N_BLK = 16


def draw_block_owner(key, part):
    key = jax.random.fold_in(key, 11)
    key_offset, key_order = jax.random.split(key)
    offsets = jax.vmap(lambda k: jax.random.permutation(k, N_BLK)[:TARGETS])(jax.random.split(key_offset, N_FSDP))
    orders = jax.vmap(lambda k: jax.random.permutation(k, BLOCKS_DEV))(jax.random.split(key_order, N_FSDP * N_BLK))
    orders = orders.reshape(N_FSDP, N_BLK, BLOCKS_DEV)
    target = orders // PER_PEER
    spread = jnp.broadcast_to(offsets[:, None, :], (N_FSDP, N_BLK, TARGETS))
    chosen = jnp.take_along_axis(spread, target, axis=2)
    sender = jnp.arange(N_BLK, dtype=jnp.int32)[None, :, None]
    owners = (sender + chosen) % N_BLK
    owners = owners.reshape(N_FSDP, N_BLK, NB_DEV, CB_DEV).transpose(1, 2, 0, 3)
    return owners.reshape(BANDS, D // BS).astype(jnp.int32)


def levels(key, dims, cuts, least, top_value):
    loudness = 1.0
    for dim, parts in cuts:
        heights = jax.random.uniform(jax.random.fold_in(jax.random.fold_in(key, 6), dim), (parts,), jnp.float32, least / len(cuts), top_value / len(cuts))
        loudness = loudness * jnp.repeat(jnp.exp(heights), dims[dim] // parts).reshape((-1,) + (1,) * (len(dims) - 1 - dim))
    return loudness


def scatter_about(stream_key, dims, scale, most, cuts=(), held_as=jnp.bfloat16):
    array = scale * jax.random.normal(stream_key, dims, jnp.float32)
    if cuts:
        array = array * levels(stream_key, dims, cuts, -0.22, 0.18)
    return jnp.clip(array, -most, most).astype(held_as)


def setup_inputs(seed: int = 0) -> dict:
    keys = jax.random.split(jax.random.key(seed), 7)
    return {
        "grad": scatter_about(keys[0], (BANDS, BS, D), 1.0, 6.0, ((0, 16), (1, 8))),
        "first_moment": scatter_about(keys[1], (N_FSDP * BLOCKS_DEV, N_BLK * BS, BS), 0.5, 4.0, ((0, 8), (1, 16))),
        "second_moment": jnp.clip(jnp.exp(math.log(2.0) - 3.6927934 * jax.random.uniform(keys[2], (N_FSDP * BLOCKS_DEV, N_BLK * BS, BS), jnp.float32) ** levels(keys[2], (N_FSDP * BLOCKS_DEV, N_BLK * BS, BS), ((0, 8), (1, 16)), -0.2, 0.2)), 0.049804688, 2.0).astype(jnp.bfloat16),
        "left_basis": scatter_about(keys[3], (N_FSDP * BLOCKS_DEV, N_BLK * BS, BS), BS ** -0.5, 0.25, ((0, 8), (1, 16))),
        "right_basis": scatter_about(keys[4], (N_FSDP * BLOCKS_DEV, N_BLK * BS, BS), BS ** -0.5, 0.25, ((0, 8), (1, 16))),
        "block_owner": draw_block_owner(jax.random.fold_in(keys[6], 71), 0),
    }


beta_one = 0.95
beta_two = 0.95
corr_value = 1.0 - 0.95 ** 10
epsilon = 1e-08

def rounded(values):
    return lax.optimization_barrier(values.astype(jnp.bfloat16)).astype(jnp.float32)

def rotate_blocks(grad_blocks, first, second, left, right):
    hp = lax.Precision.HIGHEST
    left_f = left.astype(jnp.float32)
    right_f = right.astype(jnp.float32)
    left_rotated = rounded(jnp.einsum('jia,jib->jab', left_f, grad_blocks.astype(jnp.float32), precision=hp))
    rotated = jnp.einsum('jab,jbc->jac', left_rotated, right_f, precision=hp)
    first_next = beta_one * first.astype(jnp.float32) + (1.0 - beta_one) * rotated
    second_next = beta_two * second.astype(jnp.float32) + (1.0 - beta_two) * rotated * rotated
    direction = rounded(first_next / corr_value / (jnp.sqrt(second_next / corr_value) + epsilon))
    back_left = rounded(jnp.einsum('jab,jbc->jac', left_f, direction, precision=hp))
    block_update = jnp.einsum('jac,jdc->jad', back_left, right_f, precision=hp)
    load = lax.optimization_barrier(jnp.mean(block_update * block_update, axis=(1, 2)))
    return (block_update.astype(jnp.bfloat16), first_next.astype(jnp.bfloat16), second_next.astype(jnp.bfloat16), load)

def reference(grad, first_moment, second_moment, left_basis, right_basis, block_owner):
    bands = grad.shape[0]
    columns = D // BS
    owner_flat = block_owner.reshape(bands, N_FSDP, CB_DEV).transpose(1, 0, 2).reshape(N_FSDP, bands * CB_DEV)
    hits = (owner_flat[:, :, None] == jnp.arange(N_BLK, dtype=jnp.int32)[None, None, :]).astype(jnp.int32)
    slot_flat = lax.optimization_barrier(jnp.sum((jnp.cumsum(hits, axis=1) - hits) * hits, axis=-1)).astype(jnp.int32)
    slot = slot_flat.reshape(N_FSDP, bands, CB_DEV).transpose(1, 0, 2).reshape(bands, columns)
    group = (jnp.arange(columns, dtype=jnp.int32) // CB_DEV).astype(jnp.int32)
    state_row = (group[None, :] * BLOCKS_DEV + slot).astype(jnp.int32)
    shape_four = (N_FSDP * BLOCKS_DEV, N_BLK, BS, BS)
    first_all = first_moment.reshape(shape_four)
    second_all = second_moment.reshape(shape_four)
    left_all = left_basis.reshape(shape_four)
    right_all = right_basis.reshape(shape_four)

    def per_band(items):
        band_grad, rows, owners = items
        grad_blocks = band_grad.reshape(BS, columns, BS).transpose(1, 0, 2)
        return rotate_blocks(grad_blocks, first_all[rows, owners], second_all[rows, owners], left_all[rows, owners], right_all[rows, owners])
    blocks_out, first_out, second_out, loads = lax.map(per_band, (grad, state_row, block_owner))
    update = blocks_out.transpose(0, 2, 1, 3).reshape(bands, BS, D)
    new_first = jnp.zeros(shape_four, jnp.bfloat16).at[state_row, block_owner].set(first_out)
    new_second = jnp.zeros(shape_four, jnp.bfloat16).at[state_row, block_owner].set(second_out)
    group_full = jnp.broadcast_to(group[None, :], (bands, columns))
    owner_load = jnp.zeros((N_FSDP, N_BLK), jnp.float32).at[group_full, block_owner].add(loads)
    new_first = new_first.reshape(N_FSDP * BLOCKS_DEV, N_BLK * BS, BS)
    new_second = new_second.reshape(N_FSDP * BLOCKS_DEV, N_BLK * BS, BS)
    return (update, new_first, new_second, owner_load)
```

```python
import jax
import jax.numpy as jnp
from jax import lax
from jax.experimental import pallas as pl
from jax.experimental.pallas import tpu as pltpu
from jax.sharding import PartitionSpec as P

beta_one = 0.95
beta_two = 0.95
corr_value = 1.0 - 0.95**10
epsilon = 1e-08

MESH = pl.DeviceIdType.MESH
BS = 512
SLOTS = 6
OWNERS = 16
TILES = SLOTS * OWNERS
STRIP = BS // OWNERS

BLK_STEPS = (
    (0, 1), (1, 0), (0, 3), (3, 0), (1, 2), (2, 1), (3, 2), (2, 3),
    (0, 2), (2, 0), (1, 1), (3, 3), (1, 3), (3, 1), (2, 2), (0, 0),
)
ROW_STEPS = (
    (1, 0, 0), (3, 1, 0), (2, 0, 0), (0, 1, 0), (3, 0, 1), (1, 1, 1), (0, 0, 1), (2, 1, 1),
    (1, 0, 1), (3, 1, 1), (2, 0, 1), (0, 1, 1), (3, 0, 0), (1, 1, 0), (0, 0, 0), (2, 1, 0),
)


def tables(block_owner, group):
    own = lax.dynamic_slice_in_dim(block_owner, group * 2, 2, 1).reshape(TILES)
    order = jnp.arange(TILES, dtype=jnp.int32)
    earlier = (own[:, None] == own[None, :]) & (order[None, :] < order[:, None])
    pos = jnp.sum(earlier.astype(jnp.int32), axis=1) * OWNERS + own
    src = jnp.sum(jnp.where(pos[:, None] == order[None, :], order[:, None], 0), axis=0)
    return src, pos


def kernel(
    src_ref, pos_ref, grad, first, second, left, right,
    update, new_first, new_second, load_ref,
    spread, picked, blocks, ql, qr, mom, var, out_blocks, returned, repacked,
    turned, rotated, direction, back,
    send_sem, one_sem, block_sem, state_sem, out_sem,
):
    f = lax.axis_index("fsdp")
    b = lax.axis_index("blk")
    x, c, z, y = f // 2, f % 2, b // 4, b % 4

    def row_target(step):
        dx, dc, half = step
        gx, gc = (x + dx) % 4, (c + dc) % 2
        return gx * 2 + gc, ((x - gx - 2 * gc + 8) % 4) * 4 + 2 * c + half

    def blk_target(step):
        dz, dy = step
        tz = z + dz + c * (dy - dz)
        ty = y + dy + c * (dz - dy)
        return (tz % 4) * 4 + ty % 4

    def strip_rows(middle):
        strip = ((x + 2 * c + middle // 4) % 4) * 4 + middle % 4
        return pl.ds(pl.multiple_of(strip * STRIP, STRIP), STRIP)

    home = ((x + z + 2 * c) % 4) * 2 + y // 2
    home_half = y % 2
    mine = home == f

    barrier = pltpu.get_barrier_semaphore()
    for step in BLK_STEPS[:-1]:
        pl.semaphore_signal(barrier, inc=1, device_id=(f, blk_target(step)), device_id_type=MESH)
        pl.semaphore_signal(barrier, inc=1, device_id=(home, blk_target(step)), device_id_type=MESH)

    @pl.when(jnp.logical_not(mine))
    def _():
        pl.semaphore_signal(barrier, inc=1, device_id=(home, b), device_id_type=MESH)

    for step in ROW_STEPS:
        tf, tb = row_target(step)
        if step[:2] == (0, 0):

            @pl.when((tf != f) | (tb != b))
            def _():
                pl.semaphore_signal(barrier, inc=1, device_id=(tf, tb), device_id_type=MESH)
        else:
            pl.semaphore_signal(barrier, inc=1, device_id=(tf, tb), device_id_type=MESH)
    pl.semaphore_wait(barrier, 47 - 2 * mine.astype(jnp.int32))

    @pl.loop(0, SLOTS)
    def _(p):
        band, col = p // 2, p % 2
        for step in ROW_STEPS:
            tf, tb = row_target(step)
            source = grad.at[
                band,
                pl.ds(step[2] * STRIP, STRIP),
                pl.ds(pl.multiple_of(tf * (2 * BS) + col * BS, BS), BS),
            ]
            place = spread.at[b * SLOTS + p]

            def send(source=source, place=place, tf=tf, tb=tb):
                pltpu.make_async_remote_copy(
                    source, place, send_sem.at[0], one_sem.at[0], device_id=(tf, tb), device_id_type=MESH
                ).start()

            if step[:2] == (0, 0):
                here = (tf == f) & (tb == b)
                pl.when(jnp.logical_not(here))(send)

                @pl.when(here)
                def _(source=source, place=place):
                    pltpu.make_async_copy(source, place, one_sem.at[0]).start()
            else:
                send()

    states = [
        pltpu.make_async_copy(array, held, state_sem.at[i])
        for i, (array, held) in enumerate(((left, ql), (right, qr), (first, mom), (second, var)))
    ]
    for copy in states:
        copy.start()
    pltpu.make_async_copy(spread, spread, one_sem.at[0]).wait()

    @pl.loop(0, SLOTS)
    def _(s):
        @pl.loop(0, OWNERS)
        def _(o):
            picked[s * OWNERS + o] = spread[src_ref[s * OWNERS + o]]

        rows = strip_rows(b)
        for step in BLK_STEPS[:-1]:
            target = blk_target(step)
            pltpu.make_async_remote_copy(
                picked.at[s * OWNERS + target],
                blocks.at[s, rows],
                send_sem.at[1],
                block_sem.at[s],
                device_id=(f, target),
                device_id_type=MESH,
            ).start()
        pltpu.make_async_copy(picked.at[s * OWNERS + b], blocks.at[s, rows], block_sem.at[s]).start()

    for copy in states:
        copy.wait()

    def block_step(s, total):
        pltpu.make_async_copy(blocks.at[s], blocks.at[s], block_sem.at[s]).wait()
        turned[...] = lax.dot_general(
            ql[s], blocks[s], (((0,), (0,)), ((), ())), preferred_element_type=jnp.float32
        ).astype(jnp.bfloat16)
        rotated[...] = jnp.dot(turned[...], qr[s], preferred_element_type=jnp.float32)

        @pl.loop(0, BS // 16)
        def _(i):
            rows = pl.ds(pl.multiple_of(i * 16, 16), 16)
            turn = rotated[rows]
            first_next = beta_one * mom[s, rows].astype(jnp.float32) + (1.0 - beta_one) * turn
            second_next = beta_two * var[s, rows].astype(jnp.float32) + (1.0 - beta_two) * turn * turn
            mom[s, rows] = first_next.astype(jnp.bfloat16)
            var[s, rows] = second_next.astype(jnp.bfloat16)
            direction[rows] = (
                first_next / corr_value / (jnp.sqrt(second_next / corr_value) + epsilon)
            ).astype(jnp.bfloat16)

        pltpu.make_async_copy(mom.at[s], new_first.at[s], out_sem.at[0]).start()
        pltpu.make_async_copy(var.at[s], new_second.at[s], out_sem.at[1]).start()
        back[...] = jnp.dot(ql[s], direction[...], preferred_element_type=jnp.float32).astype(jnp.bfloat16)
        for half in range(2):
            rows = pl.ds(half * 256, 256)
            done = lax.dot_general(
                back[rows], qr[s], (((1,), (1,)), ((), ())), preferred_element_type=jnp.float32
            )
            out_blocks[s, rows] = done.astype(jnp.bfloat16)
            total = total + jnp.sum((done * done).reshape(32, 8, BS), axis=0)
        for step in BLK_STEPS[:-1]:
            target = blk_target(step)
            pltpu.make_async_remote_copy(
                out_blocks.at[s, strip_rows(target)],
                returned.at[s * OWNERS + b],
                send_sem.at[2],
                one_sem.at[1],
                device_id=(f, target),
                device_id_type=MESH,
            ).start()
        pltpu.make_async_copy(
            out_blocks.at[s, strip_rows(b)],
            returned.at[s * OWNERS + b],
            one_sem.at[1],
        ).start()
        return total

    total = lax.fori_loop(0, SLOTS, block_step, jnp.zeros((8, BS), jnp.float32))
    load_ref[0, 0] = jnp.sum(total) / (BS * BS)

    pltpu.make_async_copy(returned, returned, one_sem.at[1]).wait()

    @pl.loop(0, SLOTS)
    def _(p):
        @pl.loop(0, OWNERS)
        def _(t):
            repacked[p * OWNERS + t] = returned[pos_ref[t * SLOTS + p]]

        place = update.at[
            p // 2,
            pl.ds(pl.multiple_of(home_half * STRIP, STRIP), STRIP),
            pl.ds(pl.multiple_of(f * (2 * BS) + p % 2 * BS, BS), BS),
        ]
        for step in BLK_STEPS[:-1]:
            target = blk_target(step)
            pltpu.make_async_remote_copy(
                repacked.at[p * OWNERS + target],
                place,
                send_sem.at[3],
                one_sem.at[2],
                device_id=(home, target),
                device_id_type=MESH,
            ).start()

        @pl.when(mine)
        def _():
            pltpu.make_async_copy(repacked.at[p * OWNERS + b], place, one_sem.at[2]).start()

        @pl.when(jnp.logical_not(mine))
        def _():
            pltpu.make_async_remote_copy(
                repacked.at[p * OWNERS + b],
                place,
                send_sem.at[3],
                one_sem.at[2],
                device_id=(home, b),
                device_id_type=MESH,
            ).start()

    few = spread.at[pl.ds(0, TILES - SLOTS)]
    for i in (1, 2):
        pltpu.make_async_copy(few, few, send_sem.at[i]).wait()

    @pl.when(mine)
    def _():
        for i in (0, 3):
            pltpu.make_async_copy(few, few, send_sem.at[i]).wait()

    @pl.when(jnp.logical_not(mine))
    def _():
        for i in (0, 3):
            pltpu.make_async_copy(spread, spread, send_sem.at[i]).wait()

    pltpu.make_async_copy(mom, new_first, out_sem.at[0]).wait()
    pltpu.make_async_copy(var, new_second, out_sem.at[1]).wait()
    pltpu.make_async_copy(update, update, one_sem.at[2]).wait()


def body(grad, first_moment, second_moment, left_basis, right_basis, block_owner):
    src, pos = tables(block_owner, lax.axis_index("fsdp"))
    bf = jnp.bfloat16
    state = jax.ShapeDtypeStruct(first_moment.shape, bf)
    whole = pl.BlockSpec(memory_space=pl.ANY)
    scalar = pl.BlockSpec(memory_space=pltpu.SMEM)
    strips = pltpu.VMEM((TILES, STRIP, BS), bf)
    held = pltpu.VMEM((SLOTS, BS, BS), bf)
    one = pltpu.VMEM((BS, BS), bf)
    return pl.pallas_call(
        kernel,
        out_shape=(
            jax.ShapeDtypeStruct(grad.shape, bf),
            state,
            state,
            jax.ShapeDtypeStruct((1, 1), jnp.float32),
        ),
        in_specs=[scalar] * 2 + [whole] * 5,
        out_specs=(whole, whole, whole, scalar),
        scratch_shapes=[
            strips, strips, held, held, held, held, held, held, strips, strips,
            one, pltpu.VMEM((BS, BS), jnp.float32), one, one,
            pltpu.SemaphoreType.DMA((4,)),
            pltpu.SemaphoreType.DMA((3,)),
            pltpu.SemaphoreType.DMA((SLOTS,)),
            pltpu.SemaphoreType.DMA((4,)),
            pltpu.SemaphoreType.DMA((2,)),
        ],
        compiler_params=pltpu.CompilerParams(
            collective_id=0, has_side_effects=True, vmem_limit_bytes=60 * 1024 * 1024
        ),
    )(src, pos, grad, first_moment, second_moment, left_basis, right_basis)


def solution(mesh):
    placed = (
        P("blk", "fsdp", None),
        P("fsdp", "blk", None),
        P("fsdp", "blk", None),
        P("fsdp", "blk", None),
        P("fsdp", "blk", None),
        P(),
    )
    return jax.shard_map(
        body,
        mesh=mesh,
        in_specs=placed,
        out_specs=(
            P("blk", "fsdp", None),
            P("fsdp", "blk", None),
            P("fsdp", "blk", None),
            P("fsdp", "blk"),
        ),
        check_vma=False,
    )
```

```python
import jax
import jax.numpy as jnp
from jax import lax
from jax.experimental import pallas as pl
from jax.experimental.pallas import tpu as pltpu
from jax.sharding import PartitionSpec as P

beta_one = 0.95
beta_two = 0.95
corr_value = 1.0 - 0.95**10
epsilon = 1e-08

MESH = pl.DeviceIdType.MESH
BS = 512
SLOTS = 6
OWNERS = 16
BANDS = 3 * OWNERS
TILES = SLOTS * OWNERS
STRIP = BS // OWNERS

BLK_STEPS = (
    (0, 1), (1, 0), (2, 3), (3, 2), (0, 2), (1, 1), (2, 0), (3, 3),
    (0, 3), (1, 2), (2, 1), (3, 0), (0, 0), (1, 3), (2, 2), (3, 1),
)
ROW_STEPS = (
    (0, 1, 0), (1, 0, 1), (2, 1, 0), (3, 0, 1), (0, 0, 0), (1, 1, 1), (2, 0, 0), (3, 1, 1),
    (0, 1, 1), (1, 0, 0), (2, 1, 1), (3, 0, 0), (0, 0, 1), (1, 1, 0), (2, 0, 1), (3, 1, 0),
)


def find_places(owners, table, group):
    names = owners[...]
    row_of = lax.broadcasted_iota(jnp.int32, names.shape, 0)
    bands = names.shape[1]
    sub = lax.broadcasted_iota(jnp.int32, (bands, bands), 0)
    lane = lax.broadcasted_iota(jnp.int32, (bands, bands), 1)

    def upright(row):
        return jnp.sum(jnp.where(sub == lane, row, 0), axis=1, keepdims=True)

    def count(column, row, earlier):
        return jnp.sum(jnp.where((column == row) & earlier, 1, 0), axis=0, keepdims=True)

    first, second = (
        jnp.sum(jnp.where(row_of == group * 2 + i, names, 0), axis=0, keepdims=True) for i in range(2)
    )
    first_up, second_up = upright(first), upright(second)
    place_one = first + OWNERS * (count(first_up, first, sub < lane) + count(second_up, first, sub < lane))
    place_two = second + OWNERS * (count(first_up, second, sub <= lane) + count(second_up, second, sub < lane))
    table[0:1, 0:bands] = jnp.minimum(place_one, TILES - 1)
    table[1:2, 0:bands] = jnp.minimum(place_two, TILES - 1)
    band = lax.broadcasted_iota(jnp.int32, (bands, 128), 0)
    place = lax.broadcasted_iota(jnp.int32, (bands, 128), 1)
    block = jnp.sum(
        jnp.where(upright(place_one) == place, band * 2, 0) + jnp.where(upright(place_two) == place, band * 2 + 1, 0),
        axis=0,
        keepdims=True,
    )
    table[2:3, :] = jnp.minimum(block, TILES - 1)


def kernel(
    owner_names, grad, first, second, left, right,
    update, new_first, new_second, load_ref,
    owners, table, places,
    rows_here, spread, picked, blocks, ql, qr, mom, var, out_blocks, returned, repacked,
    turned, rotated, direction, back,
    stage_sem, send_sem, one_sem, block_sem, state_sem,
):
    f = lax.axis_index("fsdp")
    b = lax.axis_index("blk")
    x, c, z, y = f // 2, f % 2, b // 4, b % 4

    def row_target(step):
        dz, parity, bit = step
        tz, half, gc = (z + dz + 2 * c) % 4, (y + parity) % 2, (y // 2 + bit) % 2
        gx = (x - tz - 2 * gc + 8) % 4
        return gx * 2 + gc, tz * 4 + 2 * c + half, half

    def blk_target(step):
        dz, dy = step
        return (z + dz + 2 * c) % 4 * 4 + (y + dy + 2 * c) % 4

    def strip_rows(middle):
        strip = ((x + 2 * c + middle // 4) % 4) * 4 + middle % 4
        return pl.ds(pl.multiple_of(strip * STRIP, STRIP), STRIP)

    home = ((x + z + 2 * c) % 4) * 2 + y // 2
    home_half = y % 2
    mine = home == f

    def unless_here(tf, tb, send, keep, always):
        if always:
            send()
            return
        here = (tf == f) & (tb == b)
        pl.when(jnp.logical_not(here))(send)
        if keep is not None:
            pl.when(here)(keep)

    def pass_on(source, place, sent, arrived, tf, tb, always):
        def send():
            pltpu.make_async_remote_copy(
                source, place, sent, arrived, device_id=(tf, tb), device_id_type=MESH
            ).start()

        def keep():
            pltpu.make_async_copy(source, place, arrived).start()

        unless_here(tf, tb, send, keep, always)

    staging = pltpu.make_async_copy(grad, rows_here, stage_sem.at[0])
    staging.start()
    barrier = pltpu.get_barrier_semaphore()

    def greet(tf, tb, always):
        def send():
            pl.semaphore_signal(barrier, inc=1, device_id=(tf, tb), device_id_type=MESH)

        unless_here(tf, tb, send, None, always)

    for step in BLK_STEPS:
        greet(f, blk_target(step), step not in ((0, 0), (2, 2)))
        greet(home, blk_target(step), step not in ((0, 0), (2, 2)))
    for step in ROW_STEPS:
        tf, tb, _ = row_target(step)
        greet(tf, tb, step[0] % 2 == 1)
    pl.semaphore_wait(barrier, 47 - 2 * mine.astype(jnp.int32))

    staging.wait()
    @pl.loop(0, SLOTS)
    def _(p):
        band, col = p // 2, p % 2
        for step in ROW_STEPS:
            tf, tb, half = row_target(step)
            source = rows_here.at[
                band,
                pl.ds(pl.multiple_of(half * STRIP, STRIP), STRIP),
                pl.ds(pl.multiple_of(tf * (2 * BS) + col * BS, BS), BS),
            ]
            pass_on(
                source, spread.at[b * SLOTS + p], send_sem.at[0], one_sem.at[0], tf, tb, step[0] % 2 == 1
            )

    states = [
        pltpu.make_async_copy(array, held, state_sem.at[i])
        for i, (array, held) in enumerate(((left, ql), (right, qr), (first, mom), (second, var)))
    ]
    copy = pltpu.make_async_copy(owner_names, owners, state_sem.at[4])
    copy.start()
    for state in states:
        state.start()
    copy.wait()
    find_places(owners, table, f)
    copy = pltpu.make_async_copy(table, places, state_sem.at[4])
    copy.start()
    copy.wait()
    pltpu.make_async_copy(spread, spread, one_sem.at[0]).wait()

    @pl.loop(0, SLOTS)
    def _(s):
        @pl.loop(0, OWNERS)
        def _(o):
            picked[s * OWNERS + o] = spread[places[2, s * OWNERS + o]]

        rows = strip_rows(b)
        for step in BLK_STEPS:
            target = blk_target(step)
            pass_on(
                picked.at[s * OWNERS + target], blocks.at[s, rows], send_sem.at[1], block_sem.at[s],
                f, target, step not in ((0, 0), (2, 2)),
            )

    for state in states:
        state.wait()

    def block_step(s, total):
        pltpu.make_async_copy(blocks.at[s], blocks.at[s], block_sem.at[s]).wait()
        turned[...] = lax.dot_general(
            ql[s], blocks[s], (((0,), (0,)), ((), ())), preferred_element_type=jnp.float32
        ).astype(jnp.bfloat16)
        rotated[...] = jnp.dot(turned[...], qr[s], preferred_element_type=jnp.float32)

        @pl.loop(0, BS // 16)
        def _(i):
            rows = pl.ds(pl.multiple_of(i * 16, 16), 16)
            turn = rotated[rows]
            first_next = beta_one * mom[s, rows].astype(jnp.float32) + (1.0 - beta_one) * turn
            second_next = beta_two * var[s, rows].astype(jnp.float32) + (1.0 - beta_two) * turn * turn
            new_first[s, rows] = first_next.astype(jnp.bfloat16)
            new_second[s, rows] = second_next.astype(jnp.bfloat16)
            direction[rows] = (
                first_next / corr_value / (jnp.sqrt(second_next / corr_value) + epsilon)
            ).astype(jnp.bfloat16)

        back[...] = jnp.dot(ql[s], direction[...], preferred_element_type=jnp.float32).astype(jnp.bfloat16)
        for half in range(2):
            rows = pl.ds(half * 256, 256)
            done = lax.dot_general(
                back[rows], qr[s], (((1,), (1,)), ((), ())), preferred_element_type=jnp.float32
            )
            out_blocks[s, rows] = done.astype(jnp.bfloat16)
            total = total + jnp.sum((done * done).reshape(32, 8, BS), axis=0)
        for step in BLK_STEPS:
            target = blk_target(step)
            pass_on(
                out_blocks.at[s, strip_rows(target)], returned.at[s * OWNERS + b], send_sem.at[2], one_sem.at[1],
                f, target, step not in ((0, 0), (2, 2)),
            )
        return total

    total = lax.fori_loop(0, SLOTS, block_step, jnp.zeros((8, BS), jnp.float32))
    load_ref[0, 0] = jnp.sum(total) / (BS * BS)

    pltpu.make_async_copy(returned, returned, one_sem.at[1]).wait()

    @pl.loop(0, SLOTS)
    def _(p):
        @pl.loop(0, OWNERS)
        def _(t):
            repacked[p * OWNERS + t] = returned[places[p % 2, t * 3 + p // 2]]

        place = update.at[
            p // 2,
            pl.ds(pl.multiple_of(home_half * STRIP, STRIP), STRIP),
            pl.ds(pl.multiple_of(f * (2 * BS) + p % 2 * BS, BS), BS),
        ]
        for step in BLK_STEPS:
            target = blk_target(step)
            pass_on(
                repacked.at[p * OWNERS + target], place, send_sem.at[3], one_sem.at[2],
                home, target, step not in ((0, 0), (2, 2)),
            )

    few = spread.at[pl.ds(0, TILES - SLOTS)]
    for i in (1, 2):
        pltpu.make_async_copy(few, few, send_sem.at[i]).wait()

    @pl.when(mine)
    def _():
        for i in (0, 3):
            pltpu.make_async_copy(few, few, send_sem.at[i]).wait()

    @pl.when(jnp.logical_not(mine))
    def _():
        for i in (0, 3):
            pltpu.make_async_copy(spread, spread, send_sem.at[i]).wait()

    pltpu.make_async_copy(update, update, one_sem.at[2]).wait()


def body(grad, first_moment, second_moment, left_basis, right_basis, block_owner):
    bf = jnp.bfloat16
    state = pltpu.VMEM(first_moment.shape, bf)
    kept = pl.BlockSpec(memory_space=pltpu.VMEM)
    whole = pl.BlockSpec(memory_space=pl.ANY)
    scalar = pl.BlockSpec(memory_space=pltpu.SMEM)
    strips = pltpu.VMEM((TILES, STRIP, BS), bf)
    held = pltpu.VMEM((SLOTS, BS, BS), bf)
    one = pltpu.VMEM((BS, BS), bf)
    return pl.pallas_call(
        kernel,
        out_shape=(
            pltpu.VMEM(grad.shape, bf),
            state,
            state,
            jax.ShapeDtypeStruct((1, 1), jnp.float32),
        ),
        in_specs=[whole] * 6,
        out_specs=(kept, kept, kept, scalar),
        scratch_shapes=[
            pltpu.VMEM((OWNERS, BANDS), jnp.int32),
            pltpu.VMEM((8, 128), jnp.int32),
            pltpu.SMEM((8, 128), jnp.int32),
            pltpu.VMEM(grad.shape, bf), strips, strips, held, held, held, held, held, held, strips, strips,
            one, pltpu.VMEM((BS, BS), jnp.float32), one, one,
            pltpu.SemaphoreType.DMA((1,)),
            pltpu.SemaphoreType.DMA((4,)),
            pltpu.SemaphoreType.DMA((3,)),
            pltpu.SemaphoreType.DMA((SLOTS,)),
            pltpu.SemaphoreType.DMA((5,)),
        ],
        compiler_params=pltpu.CompilerParams(
            collective_id=0, has_side_effects=True, vmem_limit_bytes=52 * 1024 * 1024
        ),
    )(block_owner.T, grad, first_moment, second_moment, left_basis, right_basis)


def solution(mesh):
    placed = (
        P("blk", "fsdp", None),
        P("fsdp", "blk", None),
        P("fsdp", "blk", None),
        P("fsdp", "blk", None),
        P("fsdp", "blk", None),
        P(),
    )
    return jax.shard_map(
        body,
        mesh=mesh,
        in_specs=placed,
        out_specs=(
            P("blk", "fsdp", None),
            P("fsdp", "blk", None),
            P("fsdp", "blk", None),
            P("fsdp", "blk"),
        ),
        check_vma=False,
    )
```

```python
import jax
import jax.numpy as jnp
from jax import lax
from jax.experimental import pallas as pl
from jax.experimental.pallas import tpu as pltpu
from jax.sharding import PartitionSpec as P

beta_one = 0.95
beta_two = 0.95
corr_value = 1.0 - 0.95**10
epsilon = 1e-08

MESH = pl.DeviceIdType.MESH
BS = 512
SLOTS = 6
OWNERS = 16
BANDS = 3 * OWNERS
TILES = SLOTS * OWNERS
HALVES = (pl.ds(0, 256), pl.ds(256, 256))
STRIP = BS // OWNERS

BLK_STEPS = (
    (0, 1), (1, 0), (2, 3), (3, 2), (0, 2), (1, 1), (2, 0), (3, 3),
    (0, 3), (1, 2), (2, 1), (3, 0), (0, 0), (1, 3), (2, 2), (3, 1),
)
ROW_STEPS = (
    (0, 1, 0), (1, 0, 1), (2, 1, 0), (3, 0, 1), (0, 0, 0), (1, 1, 1), (2, 0, 0), (3, 1, 1),
    (0, 1, 1), (1, 0, 0), (2, 1, 1), (3, 0, 0), (0, 0, 1), (1, 1, 0), (2, 0, 1), (3, 1, 0),
)


def find_places(owners, table, group):
    names = owners[...]
    row_of = lax.broadcasted_iota(jnp.int32, names.shape, 0)
    bands = names.shape[1]
    sub = lax.broadcasted_iota(jnp.int32, (bands, bands), 0)
    lane = lax.broadcasted_iota(jnp.int32, (bands, bands), 1)

    def upright(row):
        return jnp.sum(jnp.where(sub == lane, row, 0), axis=1, keepdims=True)

    def count(column, row, earlier):
        return jnp.sum(jnp.where((column == row) & earlier, 1, 0), axis=0, keepdims=True)

    first, second = (
        jnp.sum(jnp.where(row_of == group * 2 + i, names, 0), axis=0, keepdims=True) for i in range(2)
    )
    first_up, second_up = upright(first), upright(second)
    place_one = first + OWNERS * (count(first_up, first, sub < lane) + count(second_up, first, sub < lane))
    place_two = second + OWNERS * (count(first_up, second, sub <= lane) + count(second_up, second, sub < lane))
    table[0:1, 0:bands] = jnp.minimum(place_one, TILES - 1)
    table[1:2, 0:bands] = jnp.minimum(place_two, TILES - 1)
    band = lax.broadcasted_iota(jnp.int32, (bands, 128), 0)
    place = lax.broadcasted_iota(jnp.int32, (bands, 128), 1)
    block = jnp.sum(
        jnp.where(upright(place_one) == place, band * 2, 0) + jnp.where(upright(place_two) == place, band * 2 + 1, 0),
        axis=0,
        keepdims=True,
    )
    table[2:3, :] = jnp.minimum(block, TILES - 1)


def kernel(
    owner_names, grad, first, second, left, right,
    update, new_first, new_second, load_ref,
    owners, table, places,
    rows_here, spread_one, spread_two, picked, blocks, ql, qr, mom, var, out_blocks,
    returned_one, returned_two, repacked,
    turned, rotated, direction, back,
    stage_sem, send_sem, one_sem, block_sem, state_sem,
):
    f = lax.axis_index("fsdp")
    b = lax.axis_index("blk")
    x, c, z, y = f // 2, f % 2, b // 4, b % 4

    def row_target(step):
        dz, parity, bit = step
        tz, half, gc = (z + dz + 2 * c) % 4, (y + parity) % 2, (y // 2 + bit) % 2
        gx = (x - tz - 2 * gc + 8) % 4
        return gx * 2 + gc, tz * 4 + 2 * c + half, half

    def blk_target(step):
        dz, dy = step
        return (z + dz + 2 * c) % 4 * 4 + (y + dy + 2 * c) % 4

    def strip_rows(middle):
        strip = ((x + 2 * c + middle // 4) % 4) * 4 + middle % 4
        return pl.ds(pl.multiple_of(strip * STRIP, STRIP), STRIP)

    home = ((x + z + 2 * c) % 4) * 2 + y // 2
    home_half = y % 2
    mine = home == f

    def unless_here(tf, tb, send, keep, always):
        if always:
            send()
            return
        here = (tf == f) & (tb == b)
        pl.when(jnp.logical_not(here))(send)
        if keep is not None:
            pl.when(here)(keep)

    def pass_on(source, place, sent, arrived, tf, tb, always):
        def send():
            pltpu.make_async_remote_copy(
                source, place, sent, arrived, device_id=(tf, tb), device_id_type=MESH
            ).start()

        def keep():
            pltpu.make_async_copy(source, place, arrived).start()

        unless_here(tf, tb, send, keep, always)

    spread = (spread_one, spread_two)
    returned = (returned_one, returned_two)
    staging = pltpu.make_async_copy(grad, rows_here, stage_sem.at[0])
    staging.start()
    barrier = pltpu.get_barrier_semaphore()

    def greet(tf, tb, always):
        def send():
            pl.semaphore_signal(barrier, inc=1, device_id=(tf, tb), device_id_type=MESH)

        unless_here(tf, tb, send, None, always)

    for step in BLK_STEPS:
        greet(f, blk_target(step), step not in ((0, 0), (2, 2)))
        greet(home, blk_target(step), step not in ((0, 0), (2, 2)))
    for step in ROW_STEPS:
        tf, tb, _ = row_target(step)
        greet(tf, tb, step[0] % 2 == 1)
    pl.semaphore_wait(barrier, 47 - 2 * mine.astype(jnp.int32))

    staging.wait()
    for part in range(2):

        @pl.loop(0, SLOTS)
        def _(p):
            for step in ROW_STEPS:
                tf, tb, half = row_target(step)
                source = rows_here.at[
                    p // 2,
                    pl.ds(pl.multiple_of(half * STRIP, STRIP), STRIP),
                    pl.ds(pl.multiple_of(tf * (2 * BS) + p % 2 * BS + part * 256, 256), 256),
                ]
                pass_on(
                    source, spread[part].at[b * SLOTS + p],
                    send_sem.at[0], one_sem.at[4 * part], tf, tb, step[0] % 2 == 1,
                )

    states = [
        pltpu.make_async_copy(array, held, state_sem.at[i])
        for i, (array, held) in enumerate(((left, ql), (right, qr), (first, mom), (second, var)))
    ]
    copy = pltpu.make_async_copy(owner_names, owners, state_sem.at[4])
    copy.start()
    for state in states:
        state.start()
    copy.wait()
    find_places(owners, table, f)
    copy = pltpu.make_async_copy(table, places, state_sem.at[4])
    copy.start()
    copy.wait()
    rows = strip_rows(b)
    for half, columns in enumerate(HALVES):
        pltpu.make_async_copy(spread[half], spread[half], one_sem.at[4 * half]).wait()

        @pl.loop(0, SLOTS)
        def _(s):
            @pl.loop(0, OWNERS)
            def _(o):
                picked[s * OWNERS + o, :, columns] = spread[half][places[2, s * OWNERS + o]]

            for step in BLK_STEPS:
                target = blk_target(step)
                pass_on(
                    picked.at[s * OWNERS + target, :, columns], blocks.at[s, rows, columns],
                    send_sem.at[1], block_sem.at[s] if half else one_sem.at[5],
                    f, target, step not in ((0, 0), (2, 2)),
                )

    part = blocks.at[:, :, HALVES[0]]
    pltpu.make_async_copy(part, part, one_sem.at[5]).wait()
    for state in states:
        state.wait()

    def block_step(s, total):
        part = blocks.at[s, :, HALVES[1]]
        pltpu.make_async_copy(part, part, block_sem.at[s]).wait()
        turned[...] = lax.dot_general(
            ql[s], blocks[s], (((0,), (0,)), ((), ())), preferred_element_type=jnp.float32
        ).astype(jnp.bfloat16)
        rotated[...] = jnp.dot(turned[...], qr[s], preferred_element_type=jnp.float32)

        @pl.loop(0, BS // 16)
        def _(i):
            rows = pl.ds(pl.multiple_of(i * 16, 16), 16)
            turn = rotated[rows]
            first_next = beta_one * mom[s, rows].astype(jnp.float32) + (1.0 - beta_one) * turn
            second_next = beta_two * var[s, rows].astype(jnp.float32) + (1.0 - beta_two) * turn * turn
            new_first[s, rows] = first_next.astype(jnp.bfloat16)
            new_second[s, rows] = second_next.astype(jnp.bfloat16)
            direction[rows] = (
                first_next / corr_value / (jnp.sqrt(second_next / corr_value) + epsilon)
            ).astype(jnp.bfloat16)

        back[...] = jnp.dot(ql[s], direction[...], preferred_element_type=jnp.float32).astype(jnp.bfloat16)
        for half in range(2):
            rows = pl.ds(half * 256, 256)
            done = lax.dot_general(
                back[rows], qr[s], (((1,), (1,)), ((), ())), preferred_element_type=jnp.float32
            )
            out_blocks[s, rows] = done.astype(jnp.bfloat16)
            total = total + jnp.sum((done * done).reshape(32, 8, BS), axis=0)
        for step in BLK_STEPS:
            target = blk_target(step)
            pass_on(
                out_blocks.at[s, strip_rows(target), HALVES[0]], returned[0].at[s * OWNERS + b],
                send_sem.at[2], one_sem.at[1],
                f, target, step not in ((0, 0), (2, 2)),
            )
        return total

    total = lax.fori_loop(0, SLOTS, block_step, jnp.zeros((8, BS), jnp.float32))
    load_ref[0, 0] = jnp.sum(total) / (BS * BS)

    @pl.loop(0, SLOTS)
    def _(s):
        for step in BLK_STEPS:
            target = blk_target(step)
            pass_on(
                out_blocks.at[s, strip_rows(target), HALVES[1]], returned[1].at[s * OWNERS + b],
                send_sem.at[2], one_sem.at[3],
                f, target, step not in ((0, 0), (2, 2)),
            )

    for half, columns in enumerate(HALVES):
        pltpu.make_async_copy(returned[half], returned[half], one_sem.at[1 + 2 * half]).wait()

        @pl.loop(0, SLOTS)
        def _(p):
            @pl.loop(0, OWNERS)
            def _(t):
                repacked[t * SLOTS + p, :, columns] = returned[half][places[p % 2, t * 3 + p // 2]]

            place = update.at[
                p // 2,
                pl.ds(pl.multiple_of(home_half * STRIP, STRIP), STRIP),
                pl.ds(pl.multiple_of(f * (2 * BS) + p % 2 * BS + half * 256, 256), 256),
            ]
            for step in BLK_STEPS:
                target = blk_target(step)
                pass_on(
                    repacked.at[target * SLOTS + p, :, columns],
                    place, send_sem.at[3], one_sem.at[2],
                    home, target, step not in ((0, 0), (2, 2)),
                )

    few = blocks.at[:, pl.ds(0, BS - STRIP)]
    for i in (1, 2):
        pltpu.make_async_copy(few, few, send_sem.at[i]).wait()

    @pl.when(mine)
    def _():
        for i in (0, 3):
            pltpu.make_async_copy(few, few, send_sem.at[i]).wait()

    @pl.when(jnp.logical_not(mine))
    def _():
        for i in (0, 3):
            pltpu.make_async_copy(blocks, blocks, send_sem.at[i]).wait()

    pltpu.make_async_copy(update, update, one_sem.at[2]).wait()


def write_out(*refs):
    count = (len(refs) - 1) // 2
    parts = []
    for i, (held, out) in enumerate(zip(refs[:count], refs[count:-1])):
        size = held.shape[0] // 3
        for k in range(3):
            rows = pl.ds(k * size, size)
            parts.append(pltpu.make_async_copy(held.at[rows], out.at[rows], refs[-1].at[i * 3 + k]))
    for part in parts:
        part.start()
    for part in parts:
        part.wait()


def body(grad, first_moment, second_moment, left_basis, right_basis, block_owner):
    bf = jnp.bfloat16
    state = pltpu.VMEM(first_moment.shape, bf)
    kept = pl.BlockSpec(memory_space=pltpu.VMEM)
    whole = pl.BlockSpec(memory_space=pl.ANY)
    scalar = pl.BlockSpec(memory_space=pltpu.SMEM)
    strips = pltpu.VMEM((TILES, STRIP, BS), bf)
    halves = pltpu.VMEM((TILES, STRIP, BS // 2), bf)
    held = pltpu.VMEM((SLOTS, BS, BS), bf)
    one = pltpu.VMEM((BS, BS), bf)
    *results, load = pl.pallas_call(
        kernel,
        out_shape=(
            pltpu.VMEM(grad.shape, bf),
            state,
            state,
            jax.ShapeDtypeStruct((1, 1), jnp.float32),
        ),
        in_specs=[whole] * 6,
        out_specs=(kept, kept, kept, scalar),
        scratch_shapes=[
            pltpu.VMEM((OWNERS, BANDS), jnp.int32),
            pltpu.VMEM((8, 128), jnp.int32),
            pltpu.SMEM((8, 128), jnp.int32),
            pltpu.VMEM(grad.shape, bf), halves, halves, strips, held, held, held, held, held, held,
            halves, halves, strips,
            one, pltpu.VMEM((BS, BS), jnp.float32), one, one,
            pltpu.SemaphoreType.DMA((1,)),
            pltpu.SemaphoreType.DMA((4,)),
            pltpu.SemaphoreType.DMA((6,)),
            pltpu.SemaphoreType.DMA((SLOTS,)),
            pltpu.SemaphoreType.DMA((5,)),
        ],
        compiler_params=pltpu.CompilerParams(
            collective_id=0, has_side_effects=True, vmem_limit_bytes=52 * 1024 * 1024
        ),
    )(block_owner.T, grad, first_moment, second_moment, left_basis, right_basis)
    outs = [jax.ShapeDtypeStruct(r.shape, r.dtype) for r in results]
    written = pl.pallas_call(
        write_out,
        out_shape=outs,
        in_specs=[whole] * len(outs),
        out_specs=[whole] * len(outs),
        scratch_shapes=[pltpu.SemaphoreType.DMA((3 * len(outs),))],
        compiler_params=pltpu.CompilerParams(vmem_limit_bytes=1024 * 1024),
    )(*results)
    return (*written, load)


def solution(mesh):
    placed = (
        P("blk", "fsdp", None),
        P("fsdp", "blk", None),
        P("fsdp", "blk", None),
        P("fsdp", "blk", None),
        P("fsdp", "blk", None),
        P(),
    )
    return jax.shard_map(
        body,
        mesh=mesh,
        in_specs=placed,
        out_specs=(
            P("blk", "fsdp", None),
            P("fsdp", "blk", None),
            P("fsdp", "blk", None),
            P("fsdp", "blk"),
        ),
        check_vma=False,
    )
```

```python
import jax
import jax.numpy as jnp
from jax import lax
from jax.experimental import pallas as pl
from jax.experimental.pallas import tpu as pltpu
from jax.sharding import PartitionSpec as P

beta_one = 0.95
beta_two = 0.95
corr_value = 1.0 - 0.95**10
epsilon = 1e-08

MESH = pl.DeviceIdType.MESH
BS = 512
SLOTS = 6
OWNERS = 16
BANDS = 3 * OWNERS
TILES = SLOTS * OWNERS
HALVES = (pl.ds(0, 256), pl.ds(256, 256))
STRIP = BS // OWNERS

BLK_STEPS = (
    (0, 1), (1, 0), (2, 3), (3, 2), (0, 2), (1, 1), (2, 0), (3, 3),
    (0, 3), (1, 2), (2, 1), (3, 0), (0, 0), (1, 3), (2, 2), (3, 1),
)
ROW_STEPS = (
    (0, 1, 0), (1, 0, 1), (2, 1, 0), (3, 0, 1), (0, 0, 0), (1, 1, 1), (2, 0, 0), (3, 1, 1),
    (0, 1, 1), (1, 0, 0), (2, 1, 1), (3, 0, 0), (0, 0, 1), (1, 1, 0), (2, 0, 1), (3, 1, 0),
)


def find_places(owners, table, group):
    names = owners[...]
    row_of = lax.broadcasted_iota(jnp.int32, names.shape, 0)
    bands = names.shape[1]
    sub = lax.broadcasted_iota(jnp.int32, (bands, bands), 0)
    lane = lax.broadcasted_iota(jnp.int32, (bands, bands), 1)

    def upright(row):
        return jnp.sum(jnp.where(sub == lane, row, 0), axis=1, keepdims=True)

    def count(column, row, earlier):
        return jnp.sum(jnp.where((column == row) & earlier, 1, 0), axis=0, keepdims=True)

    first, second = (
        jnp.sum(jnp.where(row_of == group * 2 + i, names, 0), axis=0, keepdims=True) for i in range(2)
    )
    first_up, second_up = upright(first), upright(second)
    place_one = first + OWNERS * (count(first_up, first, sub < lane) + count(second_up, first, sub < lane))
    place_two = second + OWNERS * (count(first_up, second, sub <= lane) + count(second_up, second, sub < lane))
    table[0:1, 0:bands] = jnp.minimum(place_one, TILES - 1)
    table[1:2, 0:bands] = jnp.minimum(place_two, TILES - 1)
    band = lax.broadcasted_iota(jnp.int32, (bands, 128), 0)
    place = lax.broadcasted_iota(jnp.int32, (bands, 128), 1)
    block = jnp.sum(
        jnp.where(upright(place_one) == place, band * 2, 0) + jnp.where(upright(place_two) == place, band * 2 + 1, 0),
        axis=0,
        keepdims=True,
    )
    table[2:3, :] = jnp.minimum(block, TILES - 1)


def kernel(
    owner_names, grad, first, second, left, right,
    update, new_first, new_second, load_ref,
    owners, table, places,
    rows_here, spread_one, spread_two, picked, blocks, ql, qr, mom, var, out_blocks,
    returned_one, returned_two, repacked,
    turned, rotated, direction, back,
    stage_sem, send_sem, one_sem, block_sem, state_sem,
):
    f = lax.axis_index("fsdp")
    b = lax.axis_index("blk")
    x, c, z, y = f // 2, f % 2, b // 4, b % 4

    def row_target(step):
        dz, parity, bit = step
        tz, half, gc = (z + dz + 2 * c) % 4, (y + parity) % 2, (y // 2 + bit) % 2
        gx = (x - tz - 2 * gc + 8) % 4
        return gx * 2 + gc, tz * 4 + 2 * c + half, half

    def blk_target(step):
        dz, dy = step
        return (z + dz + 2 * c) % 4 * 4 + (y + dy + 2 * c) % 4

    def strip_rows(middle):
        strip = ((x + 2 * c + middle // 4) % 4) * 4 + middle % 4
        return pl.ds(pl.multiple_of(strip * STRIP, STRIP), STRIP)

    home = ((x + z + 2 * c) % 4) * 2 + y // 2
    home_half = y % 2
    mine = home == f

    row_targets = [row_target(step) for step in ROW_STEPS]
    blk_targets = [blk_target(step) for step in BLK_STEPS]

    def unless_here(tf, tb, send, keep, always):
        if always:
            send()
            return
        here = (tf == f) & (tb == b)
        pl.when(jnp.logical_not(here))(send)
        if keep is not None:
            pl.when(here)(keep)

    def pass_on(source, place, sent, arrived, tf, tb, always):
        def send():
            pltpu.make_async_remote_copy(
                source, place, sent, arrived, device_id=(tf, tb), device_id_type=MESH
            ).start()

        def keep():
            pltpu.make_async_copy(source, place, arrived).start()

        unless_here(tf, tb, send, keep, always)

    spread = (spread_one, spread_two)
    returned = (returned_one, returned_two)
    staging = pltpu.make_async_copy(grad, rows_here, stage_sem.at[0])
    staging.start()
    barrier = pltpu.get_barrier_semaphore()

    def greet(tf, tb, always):
        def send():
            pl.semaphore_signal(barrier, inc=1, device_id=(tf, tb), device_id_type=MESH)

        unless_here(tf, tb, send, None, always)

    for step, target in zip(BLK_STEPS, blk_targets):
        greet(f, target, step not in ((0, 0), (2, 2)))
        greet(home, target, step not in ((0, 0), (2, 2)))
    for step, (tf, tb, _) in zip(ROW_STEPS, row_targets):
        greet(tf, tb, step[0] % 2 == 1)
    pl.semaphore_wait(barrier, 47 - 2 * mine.astype(jnp.int32))

    staging.wait()
    for part in range(2):

        @pl.loop(0, SLOTS)
        def _(p):
            for step, (tf, tb, half) in zip(ROW_STEPS, row_targets):
                source = rows_here.at[
                    p // 2,
                    pl.ds(pl.multiple_of(half * STRIP, STRIP), STRIP),
                    pl.ds(pl.multiple_of(tf * (2 * BS) + p % 2 * BS + part * 256, 256), 256),
                ]
                pass_on(
                    source, spread[part].at[b * SLOTS + p],
                    send_sem.at[0], one_sem.at[4 * part], tf, tb, step[0] % 2 == 1,
                )

    states = [
        pltpu.make_async_copy(array, held, state_sem.at[i])
        for i, (array, held) in enumerate(((left, ql), (right, qr), (first, mom), (second, var)))
    ]
    copy = pltpu.make_async_copy(owner_names, owners, state_sem.at[4])
    copy.start()
    for state in states:
        state.start()
    copy.wait()
    find_places(owners, table, f)
    copy = pltpu.make_async_copy(table, places, state_sem.at[4])
    copy.start()
    copy.wait()
    rows = strip_rows(b)
    for half, columns in enumerate(HALVES):
        pltpu.make_async_copy(spread[half], spread[half], one_sem.at[4 * half]).wait()

        @pl.loop(0, SLOTS)
        def _(s):
            @pl.loop(0, OWNERS)
            def _(o):
                picked[s * OWNERS + o, :, columns] = spread[half][places[2, s * OWNERS + o]]

            for step, target in zip(BLK_STEPS, blk_targets):
                pass_on(
                    picked.at[s * OWNERS + target, :, columns], blocks.at[s, rows, columns],
                    send_sem.at[1], block_sem.at[s] if half else one_sem.at[5],
                    f, target, step not in ((0, 0), (2, 2)),
                )

    part = blocks.at[:, :, HALVES[0]]
    pltpu.make_async_copy(part, part, one_sem.at[5]).wait()
    for state in states:
        state.wait()

    def block_step(s, total):
        part = blocks.at[s, :, HALVES[1]]
        pltpu.make_async_copy(part, part, block_sem.at[s]).wait()
        turned[...] = lax.dot_general(
            ql[s], blocks[s], (((0,), (0,)), ((), ())), preferred_element_type=jnp.float32
        ).astype(jnp.bfloat16)
        rotated[...] = jnp.dot(turned[...], qr[s], preferred_element_type=jnp.float32)

        @pl.loop(0, BS // 16)
        def _(i):
            rows = pl.ds(pl.multiple_of(i * 16, 16), 16)
            turn = rotated[rows]
            first_next = beta_one * mom[s, rows].astype(jnp.float32) + (1.0 - beta_one) * turn
            second_next = beta_two * var[s, rows].astype(jnp.float32) + (1.0 - beta_two) * turn * turn
            new_first[s, rows] = first_next.astype(jnp.bfloat16)
            new_second[s, rows] = second_next.astype(jnp.bfloat16)
            direction[rows] = (
                first_next / corr_value / (jnp.sqrt(second_next / corr_value) + epsilon)
            ).astype(jnp.bfloat16)

        back[...] = jnp.dot(ql[s], direction[...], preferred_element_type=jnp.float32).astype(jnp.bfloat16)
        for half in range(2):
            rows = pl.ds(half * 256, 256)
            done = lax.dot_general(
                back[rows], qr[s], (((1,), (1,)), ((), ())), preferred_element_type=jnp.float32
            )
            out_blocks[s, rows] = done.astype(jnp.bfloat16)
            total = total + jnp.sum((done * done).reshape(32, 8, BS), axis=0)
        for step, target in zip(BLK_STEPS, blk_targets):
            pass_on(
                out_blocks.at[s, strip_rows(target), HALVES[0]], returned[0].at[s * OWNERS + b],
                send_sem.at[2], one_sem.at[1],
                f, target, step not in ((0, 0), (2, 2)),
            )
        return total

    total = lax.fori_loop(0, SLOTS, block_step, jnp.zeros((8, BS), jnp.float32))
    load_ref[0, 0] = jnp.sum(total) / (BS * BS)

    @pl.loop(0, SLOTS)
    def _(s):
        for step, target in zip(BLK_STEPS, blk_targets):
            pass_on(
                out_blocks.at[s, strip_rows(target), HALVES[1]], returned[1].at[s * OWNERS + b],
                send_sem.at[2], one_sem.at[3],
                f, target, step not in ((0, 0), (2, 2)),
            )

    for half, columns in enumerate(HALVES):
        pltpu.make_async_copy(returned[half], returned[half], one_sem.at[1 + 2 * half]).wait()

        @pl.loop(0, SLOTS)
        def _(p):
            @pl.loop(0, OWNERS)
            def _(t):
                repacked[t * SLOTS + p, :, columns] = returned[half][places[p % 2, t * 3 + p // 2]]

            place = update.at[
                p // 2,
                pl.ds(pl.multiple_of(home_half * STRIP, STRIP), STRIP),
                pl.ds(pl.multiple_of(f * (2 * BS) + p % 2 * BS + half * 256, 256), 256),
            ]
            for step, target in zip(BLK_STEPS, blk_targets):
                pass_on(
                    repacked.at[target * SLOTS + p, :, columns],
                    place, send_sem.at[3], one_sem.at[2],
                    home, target, step not in ((0, 0), (2, 2)),
                )

    few = blocks.at[:, pl.ds(0, BS - STRIP)]
    for i in (1, 2):
        pltpu.make_async_copy(few, few, send_sem.at[i]).wait()

    @pl.when(mine)
    def _():
        for i in (0, 3):
            pltpu.make_async_copy(few, few, send_sem.at[i]).wait()

    @pl.when(jnp.logical_not(mine))
    def _():
        for i in (0, 3):
            pltpu.make_async_copy(blocks, blocks, send_sem.at[i]).wait()

    pltpu.make_async_copy(update, update, one_sem.at[2]).wait()


def write_out(*refs):
    count = (len(refs) - 1) // 2
    parts = []
    for i, (held, out) in enumerate(zip(refs[:count], refs[count:-1])):
        size = held.shape[0] // 3
        for k in range(3):
            rows = pl.ds(k * size, size)
            parts.append(pltpu.make_async_copy(held.at[rows], out.at[rows], refs[-1].at[i * 3 + k]))
    for part in parts:
        part.start()
    for part in parts:
        part.wait()


def body(grad, first_moment, second_moment, left_basis, right_basis, block_owner):
    bf = jnp.bfloat16
    state = pltpu.VMEM(first_moment.shape, bf)
    kept = pl.BlockSpec(memory_space=pltpu.VMEM)
    whole = pl.BlockSpec(memory_space=pl.ANY)
    scalar = pl.BlockSpec(memory_space=pltpu.SMEM)
    strips = pltpu.VMEM((TILES, STRIP, BS), bf)
    halves = pltpu.VMEM((TILES, STRIP, BS // 2), bf)
    held = pltpu.VMEM((SLOTS, BS, BS), bf)
    one = pltpu.VMEM((BS, BS), bf)
    *results, load = pl.pallas_call(
        kernel,
        out_shape=(
            pltpu.VMEM(grad.shape, bf),
            state,
            state,
            jax.ShapeDtypeStruct((1, 1), jnp.float32),
        ),
        in_specs=[whole] * 6,
        out_specs=(kept, kept, kept, scalar),
        scratch_shapes=[
            pltpu.VMEM((OWNERS, BANDS), jnp.int32),
            pltpu.VMEM((8, 128), jnp.int32),
            pltpu.SMEM((8, 128), jnp.int32),
            pltpu.VMEM(grad.shape, bf), halves, halves, strips, held, held, held, held, held, held,
            halves, halves, strips,
            one, pltpu.VMEM((BS, BS), jnp.float32), one, one,
            pltpu.SemaphoreType.DMA((1,)),
            pltpu.SemaphoreType.DMA((4,)),
            pltpu.SemaphoreType.DMA((6,)),
            pltpu.SemaphoreType.DMA((SLOTS,)),
            pltpu.SemaphoreType.DMA((5,)),
        ],
        compiler_params=pltpu.CompilerParams(
            collective_id=0, has_side_effects=True, vmem_limit_bytes=52 * 1024 * 1024
        ),
    )(block_owner.T, grad, first_moment, second_moment, left_basis, right_basis)
    outs = [jax.ShapeDtypeStruct(r.shape, r.dtype) for r in results]
    written = pl.pallas_call(
        write_out,
        out_shape=outs,
        in_specs=[whole] * len(outs),
        out_specs=[whole] * len(outs),
        scratch_shapes=[pltpu.SemaphoreType.DMA((3 * len(outs),))],
        compiler_params=pltpu.CompilerParams(vmem_limit_bytes=1024 * 1024),
    )(*results)
    return (*written, load)


def solution(mesh):
    placed = (
        P("blk", "fsdp", None),
        P("fsdp", "blk", None),
        P("fsdp", "blk", None),
        P("fsdp", "blk", None),
        P("fsdp", "blk", None),
        P(),
    )
    return jax.shard_map(
        body,
        mesh=mesh,
        in_specs=placed,
        out_specs=(
            P("blk", "fsdp", None),
            P("fsdp", "blk", None),
            P("fsdp", "blk", None),
            P("fsdp", "blk"),
        ),
        check_vma=False,
    )
```

```python
import jax
import jax.numpy as jnp
from jax import lax
from jax.experimental import pallas as pl
from jax.experimental.pallas import tpu as pltpu
from jax.sharding import PartitionSpec as P

beta_one = 0.95
beta_two = 0.95
corr_value = 1.0 - 0.95**10
epsilon = 1e-08

MESH = pl.DeviceIdType.MESH
BS = 512
SLOTS = 6
OWNERS = 16
BANDS = 3 * OWNERS
TILES = SLOTS * OWNERS
HALVES = (pl.ds(0, 256), pl.ds(256, 256))
STRIP = BS // OWNERS

BLK_STEPS = (
    (0, 1), (1, 0), (2, 3), (3, 2), (0, 2), (1, 1), (2, 0), (3, 3),
    (0, 3), (1, 2), (2, 1), (3, 0), (0, 0), (1, 3), (2, 2), (3, 1),
)
ROW_STEPS = (
    (0, 1, 0), (1, 0, 1), (2, 1, 0), (3, 0, 1), (0, 0, 0), (1, 1, 1), (2, 0, 0), (3, 1, 1),
    (0, 1, 1), (1, 0, 0), (2, 1, 1), (3, 0, 0), (0, 0, 1), (1, 1, 0), (2, 0, 1), (3, 1, 0),
)


def find_places(owners, table, group):
    names = owners[...]
    row_of = lax.broadcasted_iota(jnp.int32, names.shape, 0)
    bands = names.shape[1]
    sub = lax.broadcasted_iota(jnp.int32, (bands, bands), 0)
    lane = lax.broadcasted_iota(jnp.int32, (bands, bands), 1)

    def upright(row):
        return jnp.sum(jnp.where(sub == lane, row, 0), axis=1, keepdims=True)

    def count(column, row, earlier):
        return jnp.sum(jnp.where((column == row) & earlier, 1, 0), axis=0, keepdims=True)

    first, second = (
        jnp.sum(jnp.where(row_of == group * 2 + i, names, 0), axis=0, keepdims=True) for i in range(2)
    )
    first_up, second_up = upright(first), upright(second)
    place_one = first + OWNERS * (count(first_up, first, sub < lane) + count(second_up, first, sub < lane))
    place_two = second + OWNERS * (count(first_up, second, sub <= lane) + count(second_up, second, sub < lane))
    table[0:1, 0:bands] = jnp.minimum(place_one, TILES - 1)
    table[1:2, 0:bands] = jnp.minimum(place_two, TILES - 1)
    band = lax.broadcasted_iota(jnp.int32, (bands, 128), 0)
    place = lax.broadcasted_iota(jnp.int32, (bands, 128), 1)
    block = jnp.sum(
        jnp.where(upright(place_one) == place, band * 2, 0) + jnp.where(upright(place_two) == place, band * 2 + 1, 0),
        axis=0,
        keepdims=True,
    )
    table[2:3, :] = jnp.minimum(block, TILES - 1)


def kernel(
    owner_names, grad, first, second, left, right,
    update, new_first, new_second, load_ref,
    owners, table, places,
    rows_here, spread_one, spread_two, picked, blocks, ql, qr, mom, var, out_blocks,
    returned_one, returned_two, repacked,
    turned, rotated, direction, back,
    stage_sem, send_sem, one_sem, block_sem, state_sem,
):
    f = lax.axis_index("fsdp")
    b = lax.axis_index("blk")
    x, c, z, y = f // 2, f % 2, b // 4, b % 4

    def row_target(step):
        dz, parity, bit = step
        tz, half, gc = (z + dz + 2 * c) % 4, (y + parity) % 2, (y // 2 + bit) % 2
        gx = (x - tz - 2 * gc + 8) % 4
        return gx * 2 + gc, tz * 4 + 2 * c + half, half

    def blk_target(step):
        dz, dy = step
        return (z + dz + 2 * c) % 4 * 4 + (y + dy + 2 * c) % 4

    def strip_rows(middle):
        strip = ((x + 2 * c + middle // 4) % 4) * 4 + middle % 4
        return pl.ds(pl.multiple_of(strip * STRIP, STRIP), STRIP)

    home = ((x + z + 2 * c) % 4) * 2 + y // 2
    home_half = y % 2
    mine = home == f

    row_targets = [row_target(step) for step in ROW_STEPS]
    blk_targets = [blk_target(step) for step in BLK_STEPS]

    def unless_here(tf, tb, send, keep, always):
        if always:
            send()
            return
        here = (tf == f) & (tb == b)
        pl.when(jnp.logical_not(here))(send)
        if keep is not None:
            pl.when(here)(keep)

    def pass_on(source, place, sent, arrived, tf, tb, always):
        def send():
            pltpu.make_async_remote_copy(
                source, place, sent, arrived, device_id=(tf, tb), device_id_type=MESH
            ).start()

        def keep():
            pltpu.make_async_copy(source, place, arrived).start()

        unless_here(tf, tb, send, keep, always)

    spread = (spread_one, spread_two)
    returned = (returned_one, returned_two)
    staging = pltpu.make_async_copy(grad, rows_here, stage_sem.at[0])
    staging.start()
    barrier = pltpu.get_barrier_semaphore()

    def greet(tf, tb, always):
        def send():
            pl.semaphore_signal(barrier, inc=1, device_id=(tf, tb), device_id_type=MESH)

        unless_here(tf, tb, send, None, always)

    for step, target in zip(BLK_STEPS, blk_targets):
        greet(f, target, step not in ((0, 0), (2, 2)))
        greet(home, target, step not in ((0, 0), (2, 2)))
    for step, (tf, tb, _) in zip(ROW_STEPS, row_targets):
        greet(tf, tb, step[0] % 2 == 1)
    pl.semaphore_wait(barrier, 47 - 2 * mine.astype(jnp.int32))

    staging.wait()
    for part in range(2):

        @pl.loop(0, SLOTS)
        def _(p):
            for step, (tf, tb, half) in zip(ROW_STEPS, row_targets):
                source = rows_here.at[
                    p // 2,
                    pl.ds(pl.multiple_of(half * STRIP, STRIP), STRIP),
                    pl.ds(pl.multiple_of(tf * (2 * BS) + p % 2 * BS + part * 256, 256), 256),
                ]
                pass_on(
                    source, spread[part].at[b * SLOTS + p],
                    send_sem.at[0], one_sem.at[4 * part], tf, tb, step[0] % 2 == 1,
                )

    states = [
        pltpu.make_async_copy(array, held, state_sem.at[i])
        for i, (array, held) in enumerate(((left, ql), (right, qr), (first, mom), (second, var)))
    ]
    copy = pltpu.make_async_copy(owner_names, owners, state_sem.at[4])
    copy.start()
    for state in states:
        state.start()
    copy.wait()
    find_places(owners, table, f)
    copy = pltpu.make_async_copy(table, places, state_sem.at[4])
    copy.start()
    copy.wait()
    rows = strip_rows(b)
    for half, columns in enumerate(HALVES):
        pltpu.make_async_copy(spread[half], spread[half], one_sem.at[4 * half]).wait()

        @pl.loop(0, SLOTS)
        def _(s):
            @pl.loop(0, OWNERS)
            def _(o):
                picked[s * OWNERS + o, :, columns] = spread[half][places[2, s * OWNERS + o]]

            for step, target in zip(BLK_STEPS, blk_targets):
                pass_on(
                    picked.at[s * OWNERS + target, :, columns], blocks.at[s, rows, columns],
                    send_sem.at[1], block_sem.at[s] if half else one_sem.at[5],
                    f, target, step not in ((0, 0), (2, 2)),
                )

    part = blocks.at[:, :, HALVES[0]]
    pltpu.make_async_copy(part, part, one_sem.at[5]).wait()
    for state in states:
        state.wait()

    def late(s):
        for step, target in zip(BLK_STEPS, blk_targets):
            pass_on(
                out_blocks.at[s, strip_rows(target), HALVES[1]], returned[1].at[s * OWNERS + b],
                send_sem.at[2], one_sem.at[3],
                f, target, step not in ((0, 0), (2, 2)),
            )

    def block_step(s, total):
        part = blocks.at[s, :, HALVES[1]]
        pltpu.make_async_copy(part, part, block_sem.at[s]).wait()
        turned[...] = lax.dot_general(
            ql[s], blocks[s], (((0,), (0,)), ((), ())), preferred_element_type=jnp.float32
        ).astype(jnp.bfloat16)
        rotated[...] = jnp.dot(turned[...], qr[s], preferred_element_type=jnp.float32)

        @pl.loop(0, BS // 16)
        def _(i):
            rows = pl.ds(pl.multiple_of(i * 16, 16), 16)
            turn = rotated[rows]
            first_next = beta_one * mom[s, rows].astype(jnp.float32) + (1.0 - beta_one) * turn
            second_next = beta_two * var[s, rows].astype(jnp.float32) + (1.0 - beta_two) * turn * turn
            new_first[s, rows] = first_next.astype(jnp.bfloat16)
            new_second[s, rows] = second_next.astype(jnp.bfloat16)
            direction[rows] = (
                first_next / corr_value / (jnp.sqrt(second_next / corr_value) + epsilon)
            ).astype(jnp.bfloat16)

        back[...] = jnp.dot(ql[s], direction[...], preferred_element_type=jnp.float32).astype(jnp.bfloat16)
        for half in range(2):
            rows = pl.ds(half * 256, 256)
            done = lax.dot_general(
                back[rows], qr[s], (((1,), (1,)), ((), ())), preferred_element_type=jnp.float32
            )
            out_blocks[s, rows] = done.astype(jnp.bfloat16)
            total = total + jnp.sum((done * done).reshape(32, 8, BS), axis=0)
        for step, target in zip(BLK_STEPS, blk_targets):
            pass_on(
                out_blocks.at[s, strip_rows(target), HALVES[0]], returned[0].at[s * OWNERS + b],
                send_sem.at[2], one_sem.at[1],
                f, target, step not in ((0, 0), (2, 2)),
            )
        @pl.when(s >= 3)
        def _():
            late(s - 3)

        return total

    total = lax.fori_loop(0, SLOTS, block_step, jnp.zeros((8, BS), jnp.float32))
    load_ref[0, 0] = jnp.sum(total) / (BS * BS)

    pl.loop(3, SLOTS)(late)

    for half, columns in enumerate(HALVES):
        pltpu.make_async_copy(returned[half], returned[half], one_sem.at[1 + 2 * half]).wait()

        @pl.loop(0, SLOTS)
        def _(p):
            @pl.loop(0, OWNERS)
            def _(t):
                repacked[t * SLOTS + p, :, columns] = returned[half][places[p % 2, t * 3 + p // 2]]

            place = update.at[
                p // 2,
                pl.ds(pl.multiple_of(home_half * STRIP, STRIP), STRIP),
                pl.ds(pl.multiple_of(f * (2 * BS) + p % 2 * BS + half * 256, 256), 256),
            ]
            for step, target in zip(BLK_STEPS, blk_targets):
                pass_on(
                    repacked.at[target * SLOTS + p, :, columns],
                    place, send_sem.at[3], one_sem.at[2],
                    home, target, step not in ((0, 0), (2, 2)),
                )

    few = blocks.at[:, pl.ds(0, BS - STRIP)]
    for i in (1, 2):
        pltpu.make_async_copy(few, few, send_sem.at[i]).wait()

    @pl.when(mine)
    def _():
        for i in (0, 3):
            pltpu.make_async_copy(few, few, send_sem.at[i]).wait()

    @pl.when(jnp.logical_not(mine))
    def _():
        for i in (0, 3):
            pltpu.make_async_copy(blocks, blocks, send_sem.at[i]).wait()

    pltpu.make_async_copy(update, update, one_sem.at[2]).wait()


def write_out(*refs):
    count = (len(refs) - 1) // 2
    parts = []
    for i, (held, out) in enumerate(zip(refs[:count], refs[count:-1])):
        size = held.shape[0] // 3
        for k in range(3):
            rows = pl.ds(k * size, size)
            parts.append(pltpu.make_async_copy(held.at[rows], out.at[rows], refs[-1].at[i * 3 + k]))
    for part in parts:
        part.start()
    for part in parts:
        part.wait()


def body(grad, first_moment, second_moment, left_basis, right_basis, block_owner):
    bf = jnp.bfloat16
    state = pltpu.VMEM(first_moment.shape, bf)
    kept = pl.BlockSpec(memory_space=pltpu.VMEM)
    whole = pl.BlockSpec(memory_space=pl.ANY)
    scalar = pl.BlockSpec(memory_space=pltpu.SMEM)
    strips = pltpu.VMEM((TILES, STRIP, BS), bf)
    halves = pltpu.VMEM((TILES, STRIP, BS // 2), bf)
    held = pltpu.VMEM((SLOTS, BS, BS), bf)
    one = pltpu.VMEM((BS, BS), bf)
    *results, load = pl.pallas_call(
        kernel,
        out_shape=(
            pltpu.VMEM(grad.shape, bf),
            state,
            state,
            jax.ShapeDtypeStruct((1, 1), jnp.float32),
        ),
        in_specs=[whole] * 6,
        out_specs=(kept, kept, kept, scalar),
        scratch_shapes=[
            pltpu.VMEM((OWNERS, BANDS), jnp.int32),
            pltpu.VMEM((8, 128), jnp.int32),
            pltpu.SMEM((8, 128), jnp.int32),
            pltpu.VMEM(grad.shape, bf), halves, halves, strips, held, held, held, held, held, held,
            halves, halves, strips,
            one, pltpu.VMEM((BS, BS), jnp.float32), one, one,
            pltpu.SemaphoreType.DMA((1,)),
            pltpu.SemaphoreType.DMA((4,)),
            pltpu.SemaphoreType.DMA((6,)),
            pltpu.SemaphoreType.DMA((SLOTS,)),
            pltpu.SemaphoreType.DMA((5,)),
        ],
        compiler_params=pltpu.CompilerParams(
            collective_id=0, has_side_effects=True, vmem_limit_bytes=52 * 1024 * 1024
        ),
    )(block_owner.T, grad, first_moment, second_moment, left_basis, right_basis)
    outs = [jax.ShapeDtypeStruct(r.shape, r.dtype) for r in results]
    written = pl.pallas_call(
        write_out,
        out_shape=outs,
        in_specs=[whole] * len(outs),
        out_specs=[whole] * len(outs),
        scratch_shapes=[pltpu.SemaphoreType.DMA((3 * len(outs),))],
        compiler_params=pltpu.CompilerParams(vmem_limit_bytes=1024 * 1024),
    )(*results)
    return (*written, load)


def solution(mesh):
    placed = (
        P("blk", "fsdp", None),
        P("fsdp", "blk", None),
        P("fsdp", "blk", None),
        P("fsdp", "blk", None),
        P("fsdp", "blk", None),
        P(),
    )
    return jax.shard_map(
        body,
        mesh=mesh,
        in_specs=placed,
        out_specs=(
            P("blk", "fsdp", None),
            P("fsdp", "blk", None),
            P("fsdp", "blk", None),
            P("fsdp", "blk"),
        ),
        check_vma=False,
    )
```

```python
import jax
import jax.numpy as jnp
from jax import lax
from jax.experimental import pallas as pl
from jax.experimental.pallas import tpu as pltpu
from jax.sharding import PartitionSpec as P

beta_one = 0.95
beta_two = 0.95
corr_value = 1.0 - 0.95**10
epsilon = 1e-08

MESH = pl.DeviceIdType.MESH
BS = 512
SLOTS = 6
OWNERS = 16
BANDS = 3 * OWNERS
TILES = SLOTS * OWNERS
HALVES = (pl.ds(0, 256), pl.ds(256, 256))
STRIP = BS // OWNERS

BLK_STEPS = (
    (0, 1), (1, 0), (2, 3), (3, 2), (0, 2), (1, 1), (2, 0), (3, 3),
    (0, 3), (1, 2), (2, 1), (3, 0), (0, 0), (1, 3), (2, 2), (3, 1),
)
ROW_STEPS = (
    (0, 1, 0), (1, 0, 1), (2, 1, 0), (3, 0, 1), (0, 0, 0), (1, 1, 1), (2, 0, 0), (3, 1, 1),
    (0, 1, 1), (1, 0, 0), (2, 1, 1), (3, 0, 0), (0, 0, 1), (1, 1, 0), (2, 0, 1), (3, 1, 0),
)


def find_places(owners, table, group):
    names = owners[...]
    row_of = lax.broadcasted_iota(jnp.int32, names.shape, 0)
    bands = names.shape[1]
    sub = lax.broadcasted_iota(jnp.int32, (bands, bands), 0)
    lane = lax.broadcasted_iota(jnp.int32, (bands, bands), 1)

    def upright(row):
        return jnp.sum(jnp.where(sub == lane, row, 0), axis=1, keepdims=True)

    def count(column, row, earlier):
        return jnp.sum(jnp.where((column == row) & earlier, 1, 0), axis=0, keepdims=True)

    first, second = (
        jnp.sum(jnp.where(row_of == group * 2 + i, names, 0), axis=0, keepdims=True) for i in range(2)
    )
    first_up, second_up = upright(first), upright(second)
    place_one = first + OWNERS * (count(first_up, first, sub < lane) + count(second_up, first, sub < lane))
    place_two = second + OWNERS * (count(first_up, second, sub <= lane) + count(second_up, second, sub < lane))
    table[0:1, 0:bands] = jnp.minimum(place_one, TILES - 1)
    table[1:2, 0:bands] = jnp.minimum(place_two, TILES - 1)
    band = lax.broadcasted_iota(jnp.int32, (bands, 128), 0)
    place = lax.broadcasted_iota(jnp.int32, (bands, 128), 1)
    block = jnp.sum(
        jnp.where(upright(place_one) == place, band * 2, 0) + jnp.where(upright(place_two) == place, band * 2 + 1, 0),
        axis=0,
        keepdims=True,
    )
    table[2:3, :] = jnp.minimum(block, TILES - 1)


def kernel(
    owner_names, grad, first, second, left, right,
    update, new_first, new_second, load_ref,
    owners, table, places,
    rows_here, spread_one, spread_two, picked, blocks, ql, qr, mom, var, out_blocks,
    returned_one, returned_two, repacked,
    turned, rotated, direction, back,
    stage_sem, send_sem, one_sem, block_sem, state_sem,
):
    f = lax.axis_index("fsdp")
    b = lax.axis_index("blk")
    x, c, z, y = f // 2, f % 2, b // 4, b % 4

    def row_target(step):
        dz, parity, bit = step
        tz, half, gc = (z + dz + 2 * c) % 4, (y + parity) % 2, (y // 2 + bit) % 2
        gx = (x - tz - 2 * gc + 8) % 4
        return gx * 2 + gc, tz * 4 + 2 * c + half, half

    def blk_target(step):
        dz, dy = step
        return (z + dz + 2 * c) % 4 * 4 + (y + dy + 2 * c) % 4

    def strip_rows(middle):
        strip = ((x + 2 * c + middle // 4) % 4) * 4 + middle % 4
        return pl.ds(pl.multiple_of(strip * STRIP, STRIP), STRIP)

    home = ((x + z + 2 * c) % 4) * 2 + y // 2
    home_half = y % 2
    mine = home == f

    def unless_here(tf, tb, send, keep, always):
        if always:
            send()
            return
        here = (tf == f) & (tb == b)
        pl.when(jnp.logical_not(here))(send)
        if keep is not None:
            pl.when(here)(keep)

    def pass_on(source, place, sent, arrived, tf, tb, always):
        def send():
            pltpu.make_async_remote_copy(
                source, place, sent, arrived, device_id=(tf, tb), device_id_type=MESH
            ).start()

        def keep():
            pltpu.make_async_copy(source, place, arrived).start()

        unless_here(tf, tb, send, keep, always)

    spread = (spread_one, spread_two)
    returned = (returned_one, returned_two)
    staging = pltpu.make_async_copy(grad, rows_here, stage_sem.at[0])
    staging.start()
    barrier = pltpu.get_barrier_semaphore()

    def greet(tf, tb, always):
        def send():
            pl.semaphore_signal(barrier, inc=1, device_id=(tf, tb), device_id_type=MESH)

        unless_here(tf, tb, send, None, always)

    for step in BLK_STEPS:
        greet(f, blk_target(step), step not in ((0, 0), (2, 2)))
        greet(home, blk_target(step), step not in ((0, 0), (2, 2)))
    pl.semaphore_wait(barrier, 31 - mine.astype(jnp.int32))

    staging.wait()
    for part in range(2):

        @pl.loop(0, SLOTS)
        def _(p):
            for step in ROW_STEPS:
                tf, tb, half = row_target(step)
                source = rows_here.at[
                    p // 2,
                    pl.ds(pl.multiple_of(half * STRIP, STRIP), STRIP),
                    pl.ds(pl.multiple_of(tf * (2 * BS) + p % 2 * BS + part * 256, 256), 256),
                ]
                pass_on(
                    source, spread[part].at[b * SLOTS + p],
                    send_sem.at[0], one_sem.at[4 * part], tf, tb, step[0] % 2 == 1,
                )

    states = [
        pltpu.make_async_copy(array, held, state_sem.at[i])
        for i, (array, held) in enumerate(((left, ql), (right, qr), (first, mom), (second, var)))
    ]
    copy = pltpu.make_async_copy(owner_names, owners, state_sem.at[4])
    copy.start()
    for state in states:
        state.start()
    copy.wait()
    find_places(owners, table, f)
    copy = pltpu.make_async_copy(table, places, state_sem.at[4])
    copy.start()
    copy.wait()
    rows = strip_rows(b)
    for half, columns in enumerate(HALVES):
        pltpu.make_async_copy(spread[half], spread[half], one_sem.at[4 * half]).wait()

        @pl.loop(0, SLOTS)
        def _(s):
            @pl.loop(0, OWNERS)
            def _(o):
                picked[s * OWNERS + o, :, columns] = spread[half][places[2, s * OWNERS + o]]

            for step in BLK_STEPS:
                target = blk_target(step)
                pass_on(
                    picked.at[s * OWNERS + target, :, columns], blocks.at[s, rows, columns],
                    send_sem.at[1], block_sem.at[s] if half else one_sem.at[5],
                    f, target, step not in ((0, 0), (2, 2)),
                )

    part = blocks.at[:, :, HALVES[0]]
    pltpu.make_async_copy(part, part, one_sem.at[5]).wait()
    for state in states:
        state.wait()

    def block_step(s, total):
        part = blocks.at[s, :, HALVES[1]]
        pltpu.make_async_copy(part, part, block_sem.at[s]).wait()
        turned[...] = lax.dot_general(
            ql[s], blocks[s], (((0,), (0,)), ((), ())), preferred_element_type=jnp.float32
        ).astype(jnp.bfloat16)
        rotated[...] = jnp.dot(turned[...], qr[s], preferred_element_type=jnp.float32)

        @pl.loop(0, BS // 16)
        def _(i):
            rows = pl.ds(pl.multiple_of(i * 16, 16), 16)
            turn = rotated[rows]
            first_next = beta_one * mom[s, rows].astype(jnp.float32) + (1.0 - beta_one) * turn
            second_next = beta_two * var[s, rows].astype(jnp.float32) + (1.0 - beta_two) * turn * turn
            new_first[s, rows] = first_next.astype(jnp.bfloat16)
            new_second[s, rows] = second_next.astype(jnp.bfloat16)
            direction[rows] = (
                first_next / corr_value / (jnp.sqrt(second_next / corr_value) + epsilon)
            ).astype(jnp.bfloat16)

        back[...] = jnp.dot(ql[s], direction[...], preferred_element_type=jnp.float32).astype(jnp.bfloat16)
        for half in range(2):
            rows = pl.ds(half * 256, 256)
            done = lax.dot_general(
                back[rows], qr[s], (((1,), (1,)), ((), ())), preferred_element_type=jnp.float32
            )
            out_blocks[s, rows] = done.astype(jnp.bfloat16)
            total = total + jnp.sum((done * done).reshape(32, 8, BS), axis=0)
        for step in BLK_STEPS:
            target = blk_target(step)
            pass_on(
                out_blocks.at[s, strip_rows(target), HALVES[0]], returned[0].at[s * OWNERS + b],
                send_sem.at[2], one_sem.at[1],
                f, target, step not in ((0, 0), (2, 2)),
            )
        return total

    total = lax.fori_loop(0, SLOTS, block_step, jnp.zeros((8, BS), jnp.float32))
    load_ref[0, 0] = jnp.sum(total) / (BS * BS)

    @pl.loop(0, SLOTS)
    def _(s):
        for step in BLK_STEPS:
            target = blk_target(step)
            pass_on(
                out_blocks.at[s, strip_rows(target), HALVES[1]], returned[1].at[s * OWNERS + b],
                send_sem.at[2], one_sem.at[3],
                f, target, step not in ((0, 0), (2, 2)),
            )

    for half, columns in enumerate(HALVES):
        pltpu.make_async_copy(returned[half], returned[half], one_sem.at[1 + 2 * half]).wait()

        @pl.loop(0, SLOTS)
        def _(p):
            @pl.loop(0, OWNERS)
            def _(t):
                repacked[t * SLOTS + p, :, columns] = returned[half][places[p % 2, t * 3 + p // 2]]

            place = update.at[
                p // 2,
                pl.ds(pl.multiple_of(home_half * STRIP, STRIP), STRIP),
                pl.ds(pl.multiple_of(f * (2 * BS) + p % 2 * BS + half * 256, 256), 256),
            ]
            for step in BLK_STEPS:
                target = blk_target(step)
                pass_on(
                    repacked.at[target * SLOTS + p, :, columns],
                    place, send_sem.at[3], one_sem.at[2],
                    home, target, step not in ((0, 0), (2, 2)),
                )

    few = blocks.at[:, pl.ds(0, BS - STRIP)]
    for i in (1, 2):
        pltpu.make_async_copy(few, few, send_sem.at[i]).wait()

    @pl.when(mine)
    def _():
        for i in (0, 3):
            pltpu.make_async_copy(few, few, send_sem.at[i]).wait()

    @pl.when(jnp.logical_not(mine))
    def _():
        for i in (0, 3):
            pltpu.make_async_copy(blocks, blocks, send_sem.at[i]).wait()

    pltpu.make_async_copy(update, update, one_sem.at[2]).wait()


def write_out(*refs):
    count = (len(refs) - 1) // 2
    parts = []
    for i, (held, out) in enumerate(zip(refs[:count], refs[count:-1])):
        size = held.shape[0] // 3
        for k in range(3):
            rows = pl.ds(k * size, size)
            parts.append(pltpu.make_async_copy(held.at[rows], out.at[rows], refs[-1].at[i * 3 + k]))
    for part in parts:
        part.start()
    for part in parts:
        part.wait()


def body(grad, first_moment, second_moment, left_basis, right_basis, block_owner):
    bf = jnp.bfloat16
    state = pltpu.VMEM(first_moment.shape, bf)
    kept = pl.BlockSpec(memory_space=pltpu.VMEM)
    whole = pl.BlockSpec(memory_space=pl.ANY)
    scalar = pl.BlockSpec(memory_space=pltpu.SMEM)
    strips = pltpu.VMEM((TILES, STRIP, BS), bf)
    halves = pltpu.VMEM((TILES, STRIP, BS // 2), bf)
    held = pltpu.VMEM((SLOTS, BS, BS), bf)
    one = pltpu.VMEM((BS, BS), bf)
    *results, load = pl.pallas_call(
        kernel,
        out_shape=(
            pltpu.VMEM(grad.shape, bf),
            state,
            state,
            jax.ShapeDtypeStruct((1, 1), jnp.float32),
        ),
        in_specs=[whole] * 6,
        out_specs=(kept, kept, kept, scalar),
        scratch_shapes=[
            pltpu.VMEM((OWNERS, BANDS), jnp.int32),
            pltpu.VMEM((8, 128), jnp.int32),
            pltpu.SMEM((8, 128), jnp.int32),
            pltpu.VMEM(grad.shape, bf), halves, halves, strips, held, held, held, held, held, held,
            halves, halves, strips,
            one, pltpu.VMEM((BS, BS), jnp.float32), one, one,
            pltpu.SemaphoreType.DMA((1,)),
            pltpu.SemaphoreType.DMA((4,)),
            pltpu.SemaphoreType.DMA((6,)),
            pltpu.SemaphoreType.DMA((SLOTS,)),
            pltpu.SemaphoreType.DMA((5,)),
        ],
        compiler_params=pltpu.CompilerParams(
            collective_id=0, has_side_effects=True, vmem_limit_bytes=52 * 1024 * 1024
        ),
    )(block_owner.T, grad, first_moment, second_moment, left_basis, right_basis)
    outs = [jax.ShapeDtypeStruct(r.shape, r.dtype) for r in results]
    written = pl.pallas_call(
        write_out,
        out_shape=outs,
        in_specs=[whole] * len(outs),
        out_specs=[whole] * len(outs),
        scratch_shapes=[pltpu.SemaphoreType.DMA((3 * len(outs),))],
        compiler_params=pltpu.CompilerParams(vmem_limit_bytes=1024 * 1024),
    )(*results)
    return (*written, load)


def solution(mesh):
    placed = (
        P("blk", "fsdp", None),
        P("fsdp", "blk", None),
        P("fsdp", "blk", None),
        P("fsdp", "blk", None),
        P("fsdp", "blk", None),
        P(),
    )
    return jax.shard_map(
        body,
        mesh=mesh,
        in_specs=placed,
        out_specs=(
            P("blk", "fsdp", None),
            P("fsdp", "blk", None),
            P("fsdp", "blk", None),
            P("fsdp", "blk"),
        ),
        check_vma=False,
    )
```

```python
import jax
import jax.numpy as jnp
from jax import lax
from jax.experimental import pallas as pl
from jax.experimental.pallas import tpu as pltpu
from jax.sharding import PartitionSpec as P

beta_one = 0.95
beta_two = 0.95
corr_value = 1.0 - 0.95**10
epsilon = 1e-08

MESH = pl.DeviceIdType.MESH
BS = 512
SLOTS = 6
OWNERS = 16
BANDS = 3 * OWNERS
TILES = SLOTS * OWNERS
HALVES = (pl.ds(0, 256), pl.ds(256, 256))
STRIP = BS // OWNERS

BLK_STEPS = (
    (0, 1), (1, 0), (2, 3), (3, 2), (0, 2), (1, 1), (2, 0), (3, 3),
    (0, 3), (1, 2), (2, 1), (3, 0), (0, 0), (1, 3), (2, 2), (3, 1),
)
ROW_STEPS = (
    (0, 1, 0), (1, 0, 1), (2, 1, 0), (3, 0, 1), (0, 0, 0), (1, 1, 1), (2, 0, 0), (3, 1, 1),
    (0, 1, 1), (1, 0, 0), (2, 1, 1), (3, 0, 0), (0, 0, 1), (1, 1, 0), (2, 0, 1), (3, 1, 0),
)


def find_places(owners, table, group):
    names = owners[...]
    row_of = lax.broadcasted_iota(jnp.int32, names.shape, 0)
    bands = names.shape[1]
    sub = lax.broadcasted_iota(jnp.int32, (bands, bands), 0)
    lane = lax.broadcasted_iota(jnp.int32, (bands, bands), 1)

    def upright(row):
        return jnp.sum(jnp.where(sub == lane, row, 0), axis=1, keepdims=True)

    def count(column, row, earlier):
        return jnp.sum(jnp.where((column == row) & earlier, 1, 0), axis=0, keepdims=True)

    first, second = (
        jnp.sum(jnp.where(row_of == group * 2 + i, names, 0), axis=0, keepdims=True) for i in range(2)
    )
    first_up, second_up = upright(first), upright(second)
    place_one = first + OWNERS * (count(first_up, first, sub < lane) + count(second_up, first, sub < lane))
    place_two = second + OWNERS * (count(first_up, second, sub <= lane) + count(second_up, second, sub < lane))
    table[0:1, 0:bands] = jnp.minimum(place_one, TILES - 1)
    table[1:2, 0:bands] = jnp.minimum(place_two, TILES - 1)
    band = lax.broadcasted_iota(jnp.int32, (bands, 128), 0)
    place = lax.broadcasted_iota(jnp.int32, (bands, 128), 1)
    block = jnp.sum(
        jnp.where(upright(place_one) == place, band * 2, 0) + jnp.where(upright(place_two) == place, band * 2 + 1, 0),
        axis=0,
        keepdims=True,
    )
    table[2:3, :] = jnp.minimum(block, TILES - 1)


def kernel(
    owner_names, grad, first, second, left, right,
    update, new_first, new_second, load_ref,
    owners, table, places,
    rows_here, spread_one, spread_two, picked, blocks, ql, qr, mom, var, out_blocks,
    returned_one, returned_two, repacked,
    turned, rotated, direction, back,
    stage_sem, send_sem, one_sem, block_sem, state_sem,
):
    f = lax.axis_index("fsdp")
    b = lax.axis_index("blk")
    x, c, z, y = f // 2, f % 2, b // 4, b % 4

    def row_target(step):
        dz, parity, bit = step
        tz, half, gc = (z + dz + 2 * c) % 4, (y + parity) % 2, (y // 2 + bit) % 2
        gx = (x - tz - 2 * gc + 8) % 4
        return gx * 2 + gc, tz * 4 + 2 * c + half, half

    def blk_target(step):
        dz, dy = step
        return (z + dz + 2 * c) % 4 * 4 + (y + dy + 2 * c) % 4

    def strip_rows(middle):
        strip = ((x + 2 * c + middle // 4) % 4) * 4 + middle % 4
        return pl.ds(pl.multiple_of(strip * STRIP, STRIP), STRIP)

    home = ((x + z + 2 * c) % 4) * 2 + y // 2
    home_half = y % 2
    mine = home == f

    def unless_here(tf, tb, send, keep, always):
        if always:
            send()
            return
        here = (tf == f) & (tb == b)
        pl.when(jnp.logical_not(here))(send)
        if keep is not None:
            pl.when(here)(keep)

    def pass_on(source, place, sent, arrived, tf, tb, always):
        def send():
            pltpu.make_async_remote_copy(
                source, place, sent, arrived, device_id=(tf, tb), device_id_type=MESH
            ).start()

        def keep():
            pltpu.make_async_copy(source, place, arrived).start()

        unless_here(tf, tb, send, keep, always)

    spread = (spread_one, spread_two)
    returned = (returned_one, returned_two)
    staging = pltpu.make_async_copy(grad, rows_here, stage_sem.at[0])
    staging.start()
    states = [
        pltpu.make_async_copy(array, held, state_sem.at[i])
        for i, (array, held) in enumerate(((left, ql), (right, qr), (first, mom), (second, var)))
    ]
    for state in states:
        state.start()
    barrier = pltpu.get_barrier_semaphore()

    def greet(tf, tb, always):
        def send():
            pl.semaphore_signal(barrier, inc=1, device_id=(tf, tb), device_id_type=MESH)

        unless_here(tf, tb, send, None, always)

    for step in BLK_STEPS:
        greet(f, blk_target(step), step not in ((0, 0), (2, 2)))
        greet(home, blk_target(step), step not in ((0, 0), (2, 2)))
    pl.semaphore_wait(barrier, 31 - mine.astype(jnp.int32))

    staging.wait()
    for part in range(2):

        @pl.loop(0, SLOTS)
        def _(p):
            for step in ROW_STEPS:
                tf, tb, half = row_target(step)
                source = rows_here.at[
                    p // 2,
                    pl.ds(pl.multiple_of(half * STRIP, STRIP), STRIP),
                    pl.ds(pl.multiple_of(tf * (2 * BS) + p % 2 * BS + part * 256, 256), 256),
                ]
                pass_on(
                    source, spread[part].at[b * SLOTS + p],
                    send_sem.at[0], one_sem.at[4 * part], tf, tb, step[0] % 2 == 1,
                )

    copy = pltpu.make_async_copy(owner_names, owners, state_sem.at[4])
    copy.start()
    copy.wait()
    find_places(owners, table, f)
    copy = pltpu.make_async_copy(table, places, state_sem.at[4])
    copy.start()
    copy.wait()
    rows = strip_rows(b)
    for half, columns in enumerate(HALVES):
        pltpu.make_async_copy(spread[half], spread[half], one_sem.at[4 * half]).wait()

        @pl.loop(0, SLOTS)
        def _(s):
            @pl.loop(0, OWNERS)
            def _(o):
                picked[s * OWNERS + o, :, columns] = spread[half][places[2, s * OWNERS + o]]

            for step in BLK_STEPS:
                target = blk_target(step)
                pass_on(
                    picked.at[s * OWNERS + target, :, columns], blocks.at[s, rows, columns],
                    send_sem.at[1], block_sem.at[s] if half else one_sem.at[5],
                    f, target, step not in ((0, 0), (2, 2)),
                )

    part = blocks.at[:, :, HALVES[0]]
    pltpu.make_async_copy(part, part, one_sem.at[5]).wait()
    for state in states:
        state.wait()

    def block_step(s, total):
        part = blocks.at[s, :, HALVES[1]]
        pltpu.make_async_copy(part, part, block_sem.at[s]).wait()
        turned[...] = lax.dot_general(
            ql[s], blocks[s], (((0,), (0,)), ((), ())), preferred_element_type=jnp.float32
        ).astype(jnp.bfloat16)
        rotated[...] = jnp.dot(turned[...], qr[s], preferred_element_type=jnp.float32)

        @pl.loop(0, BS // 16)
        def _(i):
            rows = pl.ds(pl.multiple_of(i * 16, 16), 16)
            turn = rotated[rows]
            first_next = beta_one * mom[s, rows].astype(jnp.float32) + (1.0 - beta_one) * turn
            second_next = beta_two * var[s, rows].astype(jnp.float32) + (1.0 - beta_two) * turn * turn
            new_first[s, rows] = first_next.astype(jnp.bfloat16)
            new_second[s, rows] = second_next.astype(jnp.bfloat16)
            direction[rows] = (
                first_next / corr_value / (jnp.sqrt(second_next / corr_value) + epsilon)
            ).astype(jnp.bfloat16)

        back[...] = jnp.dot(ql[s], direction[...], preferred_element_type=jnp.float32).astype(jnp.bfloat16)
        for half in range(2):
            rows = pl.ds(half * 256, 256)
            done = lax.dot_general(
                back[rows], qr[s], (((1,), (1,)), ((), ())), preferred_element_type=jnp.float32
            )
            out_blocks[s, rows] = done.astype(jnp.bfloat16)
            total = total + jnp.sum((done * done).reshape(32, 8, BS), axis=0)
        for step in BLK_STEPS:
            target = blk_target(step)
            pass_on(
                out_blocks.at[s, strip_rows(target), HALVES[0]], returned[0].at[s * OWNERS + b],
                send_sem.at[2], one_sem.at[1],
                f, target, step not in ((0, 0), (2, 2)),
            )
        return total

    total = lax.fori_loop(0, SLOTS, block_step, jnp.zeros((8, BS), jnp.float32))
    load_ref[0, 0] = jnp.sum(total) / (BS * BS)

    @pl.loop(0, SLOTS)
    def _(s):
        for step in BLK_STEPS:
            target = blk_target(step)
            pass_on(
                out_blocks.at[s, strip_rows(target), HALVES[1]], returned[1].at[s * OWNERS + b],
                send_sem.at[2], one_sem.at[3],
                f, target, step not in ((0, 0), (2, 2)),
            )

    for half, columns in enumerate(HALVES):
        pltpu.make_async_copy(returned[half], returned[half], one_sem.at[1 + 2 * half]).wait()

        @pl.loop(0, SLOTS)
        def _(p):
            @pl.loop(0, OWNERS)
            def _(t):
                repacked[t * SLOTS + p, :, columns] = returned[half][places[p % 2, t * 3 + p // 2]]

            place = update.at[
                p // 2,
                pl.ds(pl.multiple_of(home_half * STRIP, STRIP), STRIP),
                pl.ds(pl.multiple_of(f * (2 * BS) + p % 2 * BS + half * 256, 256), 256),
            ]
            for step in BLK_STEPS:
                target = blk_target(step)
                pass_on(
                    repacked.at[target * SLOTS + p, :, columns],
                    place, send_sem.at[3], one_sem.at[2],
                    home, target, step not in ((0, 0), (2, 2)),
                )

    few = blocks.at[:, pl.ds(0, BS - STRIP)]
    for i in (1, 2):
        pltpu.make_async_copy(few, few, send_sem.at[i]).wait()

    @pl.when(mine)
    def _():
        for i in (0, 3):
            pltpu.make_async_copy(few, few, send_sem.at[i]).wait()

    @pl.when(jnp.logical_not(mine))
    def _():
        for i in (0, 3):
            pltpu.make_async_copy(blocks, blocks, send_sem.at[i]).wait()

    pltpu.make_async_copy(update, update, one_sem.at[2]).wait()


def write_out(*refs):
    count = (len(refs) - 1) // 2
    parts = []
    for i, (held, out) in enumerate(zip(refs[:count], refs[count:-1])):
        size = held.shape[0] // 3
        for k in range(3):
            rows = pl.ds(k * size, size)
            parts.append(pltpu.make_async_copy(held.at[rows], out.at[rows], refs[-1].at[i * 3 + k]))
    for part in parts:
        part.start()
    for part in parts:
        part.wait()


def body(grad, first_moment, second_moment, left_basis, right_basis, block_owner):
    bf = jnp.bfloat16
    state = pltpu.VMEM(first_moment.shape, bf)
    kept = pl.BlockSpec(memory_space=pltpu.VMEM)
    whole = pl.BlockSpec(memory_space=pl.ANY)
    scalar = pl.BlockSpec(memory_space=pltpu.SMEM)
    strips = pltpu.VMEM((TILES, STRIP, BS), bf)
    halves = pltpu.VMEM((TILES, STRIP, BS // 2), bf)
    held = pltpu.VMEM((SLOTS, BS, BS), bf)
    one = pltpu.VMEM((BS, BS), bf)
    *results, load = pl.pallas_call(
        kernel,
        out_shape=(
            pltpu.VMEM(grad.shape, bf),
            state,
            state,
            jax.ShapeDtypeStruct((1, 1), jnp.float32),
        ),
        in_specs=[whole] * 6,
        out_specs=(kept, kept, kept, scalar),
        scratch_shapes=[
            pltpu.VMEM((OWNERS, BANDS), jnp.int32),
            pltpu.VMEM((8, 128), jnp.int32),
            pltpu.SMEM((8, 128), jnp.int32),
            pltpu.VMEM(grad.shape, bf), halves, halves, strips, held, held, held, held, held, held,
            halves, halves, strips,
            one, pltpu.VMEM((BS, BS), jnp.float32), one, one,
            pltpu.SemaphoreType.DMA((1,)),
            pltpu.SemaphoreType.DMA((4,)),
            pltpu.SemaphoreType.DMA((6,)),
            pltpu.SemaphoreType.DMA((SLOTS,)),
            pltpu.SemaphoreType.DMA((5,)),
        ],
        compiler_params=pltpu.CompilerParams(
            collective_id=0, has_side_effects=True, vmem_limit_bytes=52 * 1024 * 1024
        ),
    )(block_owner.T, grad, first_moment, second_moment, left_basis, right_basis)
    outs = [jax.ShapeDtypeStruct(r.shape, r.dtype) for r in results]
    written = pl.pallas_call(
        write_out,
        out_shape=outs,
        in_specs=[whole] * len(outs),
        out_specs=[whole] * len(outs),
        scratch_shapes=[pltpu.SemaphoreType.DMA((3 * len(outs),))],
        compiler_params=pltpu.CompilerParams(vmem_limit_bytes=1024 * 1024),
    )(*results)
    return (*written, load)


def solution(mesh):
    placed = (
        P("blk", "fsdp", None),
        P("fsdp", "blk", None),
        P("fsdp", "blk", None),
        P("fsdp", "blk", None),
        P("fsdp", "blk", None),
        P(),
    )
    return jax.shard_map(
        body,
        mesh=mesh,
        in_specs=placed,
        out_specs=(
            P("blk", "fsdp", None),
            P("fsdp", "blk", None),
            P("fsdp", "blk", None),
            P("fsdp", "blk"),
        ),
        check_vma=False,
    )
```
